128 devices in a mesh: span: 4 (over y_lo, core), ctx: 32 (over x, y_hi, z).
Axes of the slice: x: 4, y: 4 (y_hi: 2, y_lo: 2; y = y_hi * 2 + y_lo), z: 4, core: 2. Of those that a mesh axis runs over, the one named last changes fastest.
Arguments:
- queries: bfloat16 [4, 2304, 4096], P('span', 'ctx'), may hold values from -6 to 6
- key_rows: bfloat16 [4, 2304, 4096], P('span', 'ctx'), may hold values from -6 to 6
- value_rows: bfloat16 [4, 2304, 4096], P('span', 'ctx'), may hold values from -6 to 6
- noise_steps: int32 [4], replicated, may hold values from 0 to 999
- span_order: int32 [4], replicated, may hold values from 0 to 3999, as said below
- token_counts: int32 [4], replicated, may hold values from 576 to 2304, as said below
Outputs:
- attended: bfloat16 [4, 2304, 4096], P('span', 'ctx')
The draws below stay inside these ranges and needn't reach their ends.
Inputs may be any that keep to these rules, and one draw needn't show every extreme that they name: `token_counts`: some span has exactly 2304 valid tokens and some other span exactly 576. `span_order`: the positions of the 4 spans are all distinct.
All inputs are finite; a program needn't handle non-finite values.
Results may differ from the reference program's by a relative error of at most 0.006.
Values may be sent and summed in bfloat16 or wider, within the bound.
No kernel may reach another device: no remote copies, remote signals or barrier semaphores. Data moves between devices by JAX's collectives and lax.ppermute only.
A program may use at most 64 MiB of HBM per device.

```python
import math
import jax
import jax.numpy as jnp
from jax import lax

HEADS = 32
HD = 128
TOKENS = 2304
SPANS = 4


def draw_queries(key, part):
    key = jax.random.fold_in(key, 3)
    shape = (SPANS, TOKENS, HEADS * HD)
    return jnp.clip(jax.random.normal(key, shape, jnp.float32), -4.0, 4.0).astype(jnp.bfloat16)


def draw_key_rows(key, part):
    key = jax.random.fold_in(key, 5)
    shape = (SPANS, TOKENS, HEADS * HD)
    return jnp.clip(jax.random.normal(key, shape, jnp.float32), -4.0, 4.0).astype(jnp.bfloat16)


def draw_token_counts(key, part):
    key = jax.random.fold_in(key, 7)
    first, second = jax.random.split(key)
    spread = jax.random.randint(first, (SPANS,), TOKENS // 4, TOKENS + 1)
    ranks = jax.random.permutation(second, SPANS)
    spread = jnp.where(ranks == 0, TOKENS, spread)
    return jnp.where(ranks == 1, TOKENS // 4, spread).astype(jnp.int32)


def draw_span_order(key, part):
    key = jax.random.fold_in(key, 11)
    first, second = jax.random.split(key)
    places = jax.random.permutation(first, SPANS).astype(jnp.int32)
    offsets = jax.random.randint(second, (SPANS,), 0, 1000).astype(jnp.int32)
    offsets = jnp.where(places == 0, 0, offsets)
    offsets = jnp.where(places == SPANS - 1, 999, offsets)
    return (places * 1000 + offsets).astype(jnp.int32)


def plant(result, own_key, least, high):
    longest = result.shape.index(max(result.shape))
    spots = []
    for shift in (0, 1):
        where = [jax.random.randint(jax.random.fold_in(own_key, axis), (), 0, length) for axis, length in enumerate(result.shape)]
        where[longest] = (where[longest] + shift) % result.shape[longest]
        spots.append(tuple(where))
    return result.at[spots[0]].set(least).at[spots[1]].set(high)


def steps_of(own_key, shape, cuts, smallest, high):
    def one(dim, parts):
        steps = jax.random.uniform(jax.random.fold_in(jax.random.fold_in(own_key, 6), dim), (parts,), jnp.float32, smallest / len(cuts), high / len(cuts))
        return jnp.repeat(jnp.exp(steps), shape[dim] // parts).reshape((-1,) + (1,) * (len(shape) - dim - 1))

    factor_of = one(*cuts[0])
    for cut in cuts[1:]:
        factor_of = factor_of * one(*cut)
    return factor_of


def scatter_about(own_key, shape, scale, limit, cuts=(), dtype=jnp.bfloat16):
    values = jax.random.normal(own_key, shape, jnp.float32) * scale
    if len(cuts) > 0:
        values = steps_of(own_key, shape, cuts, -0.22, 0.18) * values
    return jnp.clip(values, min=-limit, max=limit).astype(dtype)


def setup_inputs(seed: int = 0) -> dict:
    key_list = jax.random.split(jax.random.key(seed), 7)
    queries = draw_queries(jax.random.fold_in(key_list[6], 71), 0)
    key_rows = draw_key_rows(jax.random.fold_in(key_list[6], 71), 0)
    value_rows = scatter_about(key_list[2], (SPANS, TOKENS, HEADS * HD), 1.0, 6.0, ((0, 4), (1, 32)))
    noise_steps = plant(jax.random.randint(key_list[3], (SPANS,), 0, 1000), jax.random.fold_in(key_list[3], 1), 0, 999).astype(jnp.int32)
    span_order = draw_span_order(jax.random.fold_in(key_list[6], 71), 0)
    token_counts = draw_token_counts(jax.random.fold_in(key_list[6], 71), 0)
    return dict(queries=queries, key_rows=key_rows, value_rows=value_rows, noise_steps=noise_steps, span_order=span_order, token_counts=token_counts)


def head_gates(noise_steps, first_head, count):
    ranks = (first_head + jnp.arange(count)).astype(jnp.float32)
    freqs = jnp.exp(-math.log(10000.0) * ranks / HEADS)
    return 1.0 + 0.5 * jnp.sin(noise_steps.astype(jnp.float32)[..., None] * freqs)

def reference(queries, key_rows, value_rows, noise_steps, span_order, token_counts):
    scale = 1.0 / math.sqrt(HD)
    shaped_q = queries.reshape(SPANS, TOKENS, HEADS, HD).transpose(0, 2, 1, 3)
    shaped_k = key_rows.reshape(SPANS * TOKENS, HEADS, HD).transpose(1, 0, 2)
    shaped_v = value_rows.reshape(SPANS * TOKENS, HEADS, HD).transpose(1, 0, 2)
    source = (jnp.arange(SPANS * TOKENS) // TOKENS).astype(jnp.int32)
    within = (jnp.arange(SPANS * TOKENS) % TOKENS).astype(jnp.int32)
    key_valid = within < token_counts[source]
    gates = head_gates(noise_steps, 0, HEADS)
    results = []
    for member in range(SPANS):
        visible = key_valid & (span_order[source] <= span_order[member])

        def one_head(operands):
            q_head, k_head, v_head = operands
            scores = jnp.dot(q_head, k_head.T, preferred_element_type=jnp.float32) * scale
            scores = jnp.where(visible[None, :], scores, -jnp.inf)
            top = lax.optimization_barrier(jnp.max(scores, axis=1, keepdims=True))
            weights = jnp.exp(scores - top)
            total = lax.optimization_barrier(jnp.sum(weights, axis=1, keepdims=True))
            mixed = jnp.dot(weights.astype(jnp.bfloat16), v_head, preferred_element_type=jnp.float32)
            return mixed / total
        per_head = lax.map(one_head, (shaped_q[member], shaped_k, shaped_v))
        gated = per_head * gates[member][:, None, None]
        row_valid = jnp.arange(TOKENS).astype(jnp.int32) < token_counts[member]
        gated = jnp.where(row_valid[None, :, None], gated, 0.0)
        results.append(gated.transpose(1, 0, 2).reshape(TOKENS, HEADS * HD).astype(jnp.bfloat16))
    return jnp.stack(results)
```

```python
import math

import jax
import jax.numpy as jnp
from jax import lax
from jax.experimental import pallas as pl
from jax.experimental.pallas import tpu as pltpu
from jax.sharding import PartitionSpec as P

HEADS = 32
HD = 128
SPANS = 4
KEY_BLOCK = 768
QUERY_TILE = 288
VMEM_BYTES = 48 * 1024 * 1024


def head_gates(noise_steps, head):
    freq = jnp.exp(-math.log(10000.0) * head.astype(jnp.float32) / HEADS)
    return 1.0 + 0.5 * jnp.sin(noise_steps.astype(jnp.float32) * freq)


def attend_kernel(meta, gates, first_ref, second_ref, q_ref, o_ref, keys, values, acc, top, sems):
    tokens = first_ref.shape[0] // SPANS
    span_rows = q_ref.shape[0] // SPANS
    core = meta[2 * SPANS]
    scale = math.log2(math.e) / math.sqrt(HD)

    def loads(key_src, value_src):
        return (
            pltpu.make_async_copy(key_src, keys, sems.at[0]),
            pltpu.make_async_copy(value_src, values.at[:, pl.ds(0, HD)], sems.at[1]),
        )

    @pl.when(core == 0)
    def _():
        for copy in loads(first_ref, second_ref):
            copy.start()

    @pl.when(core != 0)
    def _():
        for copy in loads(second_ref, first_ref):
            copy.start()

    values[:, HD:] = jnp.ones((values.shape[0], HD), values.dtype)
    for copy in loads(first_ref, second_ref):
        copy.wait()

    for e in range(SPANS):
        count = meta[SPANS + e]
        whole = count // KEY_BLOCK

        @pl.when(whole * KEY_BLOCK < count)
        def _():
            base = pl.multiple_of(e * tokens + whole * KEY_BLOCK, KEY_BLOCK)
            left = count - whole * KEY_BLOCK
            rows = pl.ds(base, KEY_BLOCK)
            valid = lax.broadcasted_iota(jnp.int32, (KEY_BLOCK, HD), 0) < left
            first_key = keys[e * tokens : e * tokens + 16, :].astype(jnp.float32)[0:1, :]
            block = keys[rows, :].astype(jnp.float32)
            keys[rows, :] = jnp.where(valid, block, first_key).astype(keys.dtype)
            mixed = values[rows, :].astype(jnp.float32)
            valid2 = lax.broadcasted_iota(jnp.int32, (KEY_BLOCK, 2 * HD), 0) < left
            values[rows, :] = jnp.where(valid2, mixed, 0.0).astype(values.dtype)

    for c in range(SPANS):
        order = meta[c]
        per_tile = tokens * QUERY_TILE // span_rows
        tiles = (meta[SPANS + c] + per_tile - 1) // per_tile

        def one_tile(t, carry, c=c, order=order):
            rows = pl.ds(pl.multiple_of(c * span_rows + t * QUERY_TILE, 16), QUERY_TILE)
            q = q_ref[rows, :]
            top[...] = jnp.full(top.shape, -1e30, jnp.float32)
            acc[...] = jnp.zeros(acc.shape, jnp.float32)
            for e in range(SPANS):
                blocks = jnp.where(
                    meta[e] <= order, (meta[SPANS + e] + KEY_BLOCK - 1) // KEY_BLOCK, 0
                )

                def one_block(b, carry, e=e):
                    part = pl.ds(pl.multiple_of(e * tokens + b * KEY_BLOCK, KEY_BLOCK), KEY_BLOCK)
                    scores = lax.dot_general(
                        q, keys[part, :], (((1,), (1,)), ((), ())),
                        preferred_element_type=jnp.float32,
                    ) * scale
                    old = top[...]
                    new = jnp.maximum(old, jnp.max(scores, axis=1, keepdims=True))
                    top[...] = new
                    weights = jnp.exp2(scores - new).astype(jnp.bfloat16)
                    mixed = jnp.dot(weights, values[part, :], preferred_element_type=jnp.float32)
                    acc[...] = acc[...] * jnp.exp2(old - new) + mixed
                    return carry

                lax.fori_loop(0, blocks, one_block, 0)
            o_ref[rows, :] = (acc[:, :HD] * (gates[c] / acc[:, HD:])).astype(o_ref.dtype)
            return carry

        lax.fori_loop(0, tiles, one_tile, 0)


def attend(first, second, q, meta, gates):
    return pl.pallas_call(
        attend_kernel,
        out_shape=jax.ShapeDtypeStruct(q.shape, q.dtype),
        in_specs=[
            pl.BlockSpec(memory_space=pltpu.SMEM),
            pl.BlockSpec(memory_space=pltpu.SMEM),
            pl.BlockSpec(memory_space=pl.ANY),
            pl.BlockSpec(memory_space=pl.ANY),
            pl.BlockSpec(memory_space=pltpu.VMEM),
        ],
        out_specs=pl.BlockSpec(memory_space=pltpu.VMEM),
        scratch_shapes=[
            pltpu.VMEM(first.shape, first.dtype),
            pltpu.VMEM((first.shape[0], 2 * HD), first.dtype),
            pltpu.VMEM((QUERY_TILE, 2 * HD), jnp.float32),
            pltpu.VMEM((QUERY_TILE, 1), jnp.float32),
            pltpu.SemaphoreType.DMA((2,)),
        ],
        compiler_params=pltpu.CompilerParams(vmem_limit_bytes=VMEM_BYTES),
        name="attend",
    )(meta, gates, first, second, q)


def turned(x, axis, start, length):
    return lax.dynamic_slice_in_dim(jnp.concatenate([x, x], axis=axis), start, length, axis=axis)


def shards(queries, key_rows, value_rows, noise_steps, span_order, token_counts):
    both = ("span", "ctx")
    tok = queries.shape[1]
    piece = tok // 3
    ctx_size = lax.axis_size("ctx")
    groups = ctx_size // SPANS
    me = lax.axis_index("span")
    place = lax.axis_index("ctx")
    turn = place % SPANS
    core = me % 2

    def by_head(x):
        return x.reshape(tok, HEADS, HD).transpose(1, 0, 2)

    keys, values = by_head(key_rows), by_head(value_rows)
    q3 = by_head(queries).reshape(HEADS, 3, piece, HD).transpose(1, 0, 2, 3)
    q4 = jnp.concatenate([q3, q3[:1]], axis=0)
    q4 = turned(q4, 0, SPANS - 1 - turn, SPANS)
    kv = jnp.stack([keys, values, keys, values])
    outgoing = jnp.concatenate([kv, q4], axis=2).reshape(SPANS * HEADS, tok + piece, HD)
    incoming = lax.all_to_all(outgoing, both, split_axis=0, concat_axis=0, tiled=True)

    first = incoming[:, :tok].reshape(SPANS * ctx_size * tok, HD)
    second = lax.ppermute(first, "span", [(0, 1), (1, 0), (2, 3), (3, 2)])
    q = incoming[:, tok:].reshape(SPANS, groups, SPANS, piece, HD)
    q = turned(q, 2, me + 1, 3).reshape(SPANS * groups * 3 * piece, HD)
    gates = head_gates(noise_steps, place)
    meta = jnp.concatenate([span_order, token_counts, core[None]]).astype(jnp.int32)
    out = attend(first, second, q, meta, gates)

    out = out.reshape(SPANS, groups, 3, piece, HD)
    out = jnp.concatenate([out, out[:, :, :1]], axis=2)
    out = turned(out, 2, SPANS - 1 - me, SPANS).reshape(SPANS * ctx_size, piece, HD)
    back = lax.all_to_all(out, both, split_axis=0, concat_axis=0, tiled=True)
    back = turned(back.reshape(SPANS, HEADS, piece, HD), 0, turn + 1, 3)
    back = back.transpose(0, 2, 1, 3).reshape(tok, HEADS * HD)
    token = place * tok + jnp.arange(tok)
    back = jnp.where((token < token_counts[me])[:, None], back, jnp.zeros((), back.dtype))
    return back[None]


def solution(mesh):
    tokens = P("span", "ctx", None)
    return jax.shard_map(
        shards,
        mesh=mesh,
        in_specs=(tokens, tokens, tokens, P(), P(), P()),
        out_specs=tokens,
        check_vma=False,
    )
```

```python
import functools
import math

import jax
import jax.numpy as jnp
from jax import lax
from jax.experimental import pallas as pl
from jax.experimental.pallas import tpu as pltpu
from jax.sharding import PartitionSpec as P

HEADS = 32
HD = 128
SPANS = 4
KEY_BLOCK = 768
EDGE_ROWS = 128
QUERY_TILE = 144
GROUP = 4
PACK_HEADS = 8
VMEM_BYTES = 48 * 1024 * 1024


def head_gates(noise_steps, head):
    freq = jnp.exp(-math.log(10000.0) * head.astype(jnp.float32) / HEADS)
    return 1.0 + 0.5 * jnp.sin(noise_steps.astype(jnp.float32) * freq)


def pack_kernel(turn_ref, q_ref, k_ref, v_ref, o_ref):
    piece = q_ref.shape[0] // 3
    turn = turn_ref[0]
    for head in range(PACK_HEADS):
        columns = slice(head * HD, (head + 1) * HD)
        q = q_ref[:, columns].astype(jnp.float32)
        pieces = [q[n * piece : (n + 1) * piece] for n in range(3)]
        sides = [ref[:, columns].astype(jnp.float32) for ref in (k_ref, v_ref)]
        for member in range(SPANS):
            which = (member + SPANS - 1 - turn) % SPANS
            chosen = jnp.where(which == 0, pieces[0], jnp.where(which == 1, pieces[1], pieces[2]))
            chunk = jnp.concatenate([sides[member % 2], chosen], axis=0)
            o_ref[member, head] = chunk.astype(o_ref.dtype)


def pack(turn, q, k, v):
    tok = q.shape[0]
    columns = pl.BlockSpec((tok, PACK_HEADS * HD), lambda n: (0, n))
    return pl.pallas_call(
        pack_kernel,
        grid=(HEADS // PACK_HEADS,),
        out_shape=jax.ShapeDtypeStruct((SPANS, HEADS, tok + tok // 3, HD), q.dtype),
        in_specs=[pl.BlockSpec(memory_space=pltpu.SMEM), columns, columns, columns],
        out_specs=pl.BlockSpec((SPANS, PACK_HEADS, tok + tok // 3, HD), lambda n: (0, n, 0, 0)),
        name="pack",
    )(turn, q, k, v)


def attend_kernel(
    meta, gates, first_ref, second_ref, incoming_ref, o_ref,
    keys, values, arrived, queries, scores, weights, scales, acc, top, results, items, sems,
):
    sources, piece = o_ref.shape[0] // SPANS, o_ref.shape[1]
    tokens = first_ref.shape[0] // SPANS
    tail = arrived.shape[1]
    span_rows = tokens // SPANS
    span_tiles = span_rows // QUERY_TILE
    core, member = meta[2 * SPANS], meta[2 * SPANS + 1]
    scale = math.log2(math.e) / math.sqrt(HD)

    def loads(key_src, value_src):
        rows = pl.ds(incoming_ref.shape[1] - tail, tail)
        return (
            pltpu.make_async_copy(incoming_ref.at[:, rows, :], arrived, sems.at[2]),
            pltpu.make_async_copy(key_src, keys, sems.at[0]),
            pltpu.make_async_copy(value_src, values.at[:, pl.ds(0, HD)], sems.at[1]),
        )

    @pl.when(core == 0)
    def _():
        for copy in loads(first_ref, second_ref):
            copy.start()

    @pl.when(core != 0)
    def _():
        for copy in loads(second_ref, first_ref):
            copy.start()

    def item(tile, block, span, flag):
        return tile + (block << 8) + (span << 16) + (flag << 20)

    idle = item(SPANS * span_tiles, 0, 0, 1)
    at = jnp.int32(GROUP)
    for extra in range(GROUP):
        items[extra] = idle
    per_tile = tokens * QUERY_TILE // span_rows
    span_blocks = tokens // KEY_BLOCK
    blocks = [(meta[SPANS + e] + KEY_BLOCK - 1) // KEY_BLOCK for e in range(SPANS)]
    for c in range(SPANS):
        tiles = (meta[SPANS + c] + per_tile - 1) // per_tile
        seen = [jnp.where(meta[e] <= meta[c], blocks[e], 0) for e in range(SPANS)]

        def tile_items(t, at, c=c, seen=seen):
            start = at
            for e in range(SPANS):

                def block_item(b, at, e=e):
                    flag = jnp.where(at == start, 1, 0)
                    items[at] = item(c * span_tiles + t, e * span_blocks + b, c, flag)
                    return at + 1

                at = lax.fori_loop(0, seen[e], block_item, at)
            items[at - 1] = items[at - 1] + (2 << 20)
            return at

        at = lax.fori_loop(0, tiles, tile_items, at)
    for extra in range(4 * GROUP):
        items[at + extra] = idle

    values[:, HD:] = jnp.ones((values.shape[0], HD), values.dtype)
    for copy in loads(first_ref, second_ref):
        copy.wait()

    per_load = QUERY_TILE // (3 * piece)

    def gather_tile(t, carry):
        rows = []
        for n in range(per_load):
            for k in range(3):
                source = (t * per_load + n) * SPANS + (member + 1 + k) % SPANS
                rows.append(arrived[source].astype(jnp.float32)[tail - piece :])
        here = pl.ds(pl.multiple_of(t * QUERY_TILE, 16), QUERY_TILE)
        queries[here, :] = jnp.concatenate(rows, axis=0).astype(queries.dtype)
        return carry

    lax.fori_loop(0, SPANS * span_tiles, gather_tile, 0)

    for e in range(SPANS):
        count = meta[SPANS + e]
        first_key = keys[e * tokens : e * tokens + 16, :].astype(jnp.float32)[0:1, :]

        def edge(s, carry, e=e, count=count, first_key=first_key):
            rows = pl.ds(pl.multiple_of(e * tokens + s * EDGE_ROWS, EDGE_ROWS), EDGE_ROWS)
            left = count - s * EDGE_ROWS
            valid = lax.broadcasted_iota(jnp.int32, (EDGE_ROWS, HD), 0) < left
            block = keys[rows, :].astype(jnp.float32)
            keys[rows, :] = jnp.where(valid, block, first_key).astype(keys.dtype)
            for side in range(2):
                columns = slice(side * HD, (side + 1) * HD)
                mixed = values[rows, columns].astype(jnp.float32)
                values[rows, columns] = jnp.where(valid, mixed, 0.0).astype(values.dtype)
            return carry

        lax.fori_loop(count // EDGE_ROWS, blocks[e] * (KEY_BLOCK // EDGE_ROWS), edge, 0)

    def key_rows(i):
        return pl.ds(pl.multiple_of((items[i] >> 8 & 255) * KEY_BLOCK, KEY_BLOCK), KEY_BLOCK)

    def score(i, out):
        tile = jnp.minimum(items[i] & 255, SPANS * span_tiles - 1)
        q = queries[pl.ds(pl.multiple_of(tile * QUERY_TILE, 16), QUERY_TILE), :]
        x = lax.dot_general(
            q, keys[key_rows(i), :], (((1,), (1,)), ((), ())), preferred_element_type=jnp.float32
        )
        out[...] = x * scale

    def weigh(i, score_ref, weight_ref, scale_ref):
        parts = [score_ref[:, n * HD : (n + 1) * HD] for n in range(KEY_BLOCK // HD)]
        old = jnp.where((items[i] >> 20) & 1 == 1, -1e30, top[...])
        high = functools.reduce(jnp.maximum, parts)
        new = jnp.maximum(old, jnp.max(high, axis=1, keepdims=True))
        top[...] = new
        scale_ref[...] = jnp.exp2(old - new)
        for n, part in enumerate(parts):
            weight_ref[:, n * HD : (n + 1) * HD] = jnp.exp2(part - new).astype(jnp.bfloat16)

    def mix(i, weight_ref, scale_ref):
        mixed = jnp.dot(weight_ref[...], values[key_rows(i), :], preferred_element_type=jnp.float32)
        factor = scale_ref[...]
        sums = acc[:, :HD] * factor + mixed[:, :HD]
        totals = acc[:, HD:] * factor + mixed[:, HD:]
        acc[:, :HD] = sums
        acc[:, HD:] = totals
        rows = pl.ds(pl.multiple_of((items[i] & 255) * QUERY_TILE, 16), QUERY_TILE)
        results[rows, :] = sums * (gates[items[i] >> 16 & 3] / totals)

    acc[...] = jnp.ones(acc.shape, acc.dtype)
    top[...] = jnp.zeros(top.shape, top.dtype)
    for g in range(GROUP):
        weights[g][...] = jnp.ones(weights[g].shape, weights[g].dtype)
        scales[g][...] = jnp.zeros(scales[g].shape, scales[g].dtype)
        score(GROUP + g, scores[GROUP + g])

    def two_steps(j, carry):
        for half in range(2):
            here, there = (half + 1) % 2 * GROUP, half * GROUP
            first = (2 * j + half) * GROUP
            for g in range(GROUP):
                score(first + 2 * GROUP + g, scores[there + g])
            for g in range(GROUP):
                weigh(first + GROUP + g, scores[here + g], weights[here + g], scales[here + g])
            for g in range(GROUP):
                mix(first + g, weights[there + g], scales[there + g])
        return carry

    lax.fori_loop(0, (at + 2 * GROUP - 1) // (2 * GROUP), two_steps, 0)

    def hand_back(t, carry):
        for k in range(3):
            rows = pl.ds(pl.multiple_of((t * 3 + k) * piece, 8), piece)
            o_ref[t * SPANS + (member + 1 + k) % SPANS] = results[rows, :].astype(o_ref.dtype)
        return carry

    lax.fori_loop(0, SPANS * sources // SPANS, hand_back, 0)


def attend(first, second, incoming, meta, gates):
    chunks, rows, _ = incoming.shape
    tok = first.shape[0] // chunks
    piece = rows - tok
    total = first.shape[0] // SPANS
    tail = -(-piece // 16) * 16
    smem, anywhere = pl.BlockSpec(memory_space=pltpu.SMEM), pl.BlockSpec(memory_space=pl.ANY)
    tile = (QUERY_TILE, KEY_BLOCK)
    return pl.pallas_call(
        attend_kernel,
        out_shape=jax.ShapeDtypeStruct((chunks, piece, HD), first.dtype),
        in_specs=[smem, smem, anywhere, anywhere, anywhere],
        out_specs=pl.BlockSpec(memory_space=pltpu.VMEM),
        scratch_shapes=[
            pltpu.VMEM(first.shape, first.dtype),
            pltpu.VMEM((first.shape[0], 2 * HD), first.dtype),
            pltpu.VMEM((chunks, tail, HD), first.dtype),
            pltpu.VMEM((total, HD), first.dtype),
            [pltpu.VMEM(tile, jnp.float32)] * (2 * GROUP),
            [pltpu.VMEM(tile, jnp.bfloat16)] * (2 * GROUP),
            [pltpu.VMEM((QUERY_TILE, HD), jnp.float32)] * (2 * GROUP),
            pltpu.VMEM((QUERY_TILE, 2 * HD), jnp.float32),
            pltpu.VMEM((QUERY_TILE, HD), jnp.float32),
            pltpu.VMEM((total + QUERY_TILE, HD), jnp.float32),
            pltpu.SMEM((512,), jnp.int32),
            pltpu.SemaphoreType.DMA((3,)),
        ],
        compiler_params=pltpu.CompilerParams(vmem_limit_bytes=VMEM_BYTES),
        name="attend",
    )(meta, gates, first, second, incoming)


def turned(x, axis, start, length):
    return lax.dynamic_slice_in_dim(jnp.concatenate([x, x], axis=axis), start, length, axis=axis)


def shards(queries, key_rows, value_rows, noise_steps, span_order, token_counts):
    both = ("span", "ctx")
    tok = queries.shape[1]
    piece = tok // 3
    ctx_size = lax.axis_size("ctx")
    me = lax.axis_index("span")
    place = lax.axis_index("ctx")
    turn = place % SPANS
    core = me % 2

    outgoing = pack(turn[None], queries[0], key_rows[0], value_rows[0])
    outgoing = outgoing.reshape(SPANS * HEADS, tok + piece, HD)
    incoming = lax.all_to_all(outgoing, both, split_axis=0, concat_axis=0, tiled=True)

    first = incoming[:, :tok].reshape(SPANS * ctx_size * tok, HD)
    second = lax.ppermute(first, "span", [(0, 1), (1, 0), (2, 3), (3, 2)])
    gates = head_gates(noise_steps, place)
    meta = jnp.concatenate([span_order, token_counts, core[None], me[None]]).astype(jnp.int32)
    out = attend(first, second, incoming, meta, gates)

    back = lax.all_to_all(out, both, split_axis=0, concat_axis=0, tiled=True)
    back = turned(back.reshape(SPANS, HEADS, piece, HD), 0, turn + 1, 3)
    back = back.transpose(0, 2, 1, 3).reshape(tok, HEADS * HD)
    token = place * tok + jnp.arange(tok)
    back = jnp.where((token < token_counts[me])[:, None], back, jnp.zeros((), back.dtype))
    return back[None]


def solution(mesh):
    tokens = P("span", "ctx", None)
    return jax.shard_map(
        shards,
        mesh=mesh,
        in_specs=(tokens, tokens, tokens, P(), P(), P()),
        out_specs=tokens,
        check_vma=False,
    )
```

```python
import functools
import math

import jax
import jax.numpy as jnp
from jax import lax
from jax.experimental import pallas as pl
from jax.experimental.pallas import tpu as pltpu
from jax.sharding import PartitionSpec as P

HEADS = 32
HD = 128
SPANS = 4
KEY_BLOCK = 768
EDGE_ROWS = 128
QUERY_TILE = 144
GROUP = 4
PACK_HEADS = 16
ITEMS = 512
VMEM_BYTES = 48 * 1024 * 1024


def head_gates(noise_steps, head):
    freq = jnp.exp(-math.log(10000.0) * head.astype(jnp.float32) / HEADS)
    return 1.0 + 0.5 * jnp.sin(noise_steps.astype(jnp.float32) * freq)


def pack_kernel(turn_ref, q_ref, k_ref, v_ref, o_ref):
    piece = q_ref.shape[0] // 3
    turn = turn_ref[0]
    for head in range(PACK_HEADS):
        columns = slice(head * HD, (head + 1) * HD)
        q = q_ref[:, columns].astype(jnp.float32)
        pieces = [q[n * piece : (n + 1) * piece] for n in range(3)]
        sides = [ref[:, columns].astype(jnp.float32) for ref in (k_ref, v_ref)]
        for member in range(SPANS):
            which = (member + SPANS - 1 - turn) % SPANS
            chosen = jnp.where(which == 0, pieces[0], jnp.where(which == 1, pieces[1], pieces[2]))
            chunk = jnp.concatenate([sides[member % 2], chosen], axis=0)
            o_ref[member, head] = chunk.astype(o_ref.dtype)


def pack(turn, q, k, v):
    tok = q.shape[0]
    columns = pl.BlockSpec((tok, PACK_HEADS * HD), lambda n: (0, n))
    return pl.pallas_call(
        pack_kernel,
        grid=(HEADS // PACK_HEADS,),
        out_shape=jax.ShapeDtypeStruct((SPANS, HEADS, tok + tok // 3, HD), q.dtype),
        in_specs=[pl.BlockSpec(memory_space=pltpu.SMEM), columns, columns, columns],
        out_specs=pl.BlockSpec((SPANS, PACK_HEADS, tok + tok // 3, HD), lambda n: (0, n, 0, 0)),
        name="pack",
    )(turn, q, k, v)


def prepare_kernel(meta, incoming_ref, queries, items):
    tokens = queries.shape[0]
    piece = tokens // (3 * incoming_ref.shape[0] // SPANS)
    skipped = incoming_ref.shape[1] - piece
    span_tiles = tokens // SPANS // QUERY_TILE
    member = meta[2 * SPANS + 1]

    def item(tile, block, span, flag):
        return tile + (block << 8) + (span << 16) + (flag << 20)

    idle = item(SPANS * span_tiles, 0, 0, 1)
    at = jnp.int32(GROUP)
    for extra in range(GROUP):
        items[extra] = idle
    per_tile = SPANS * QUERY_TILE
    span_blocks = tokens // KEY_BLOCK
    blocks = [(meta[SPANS + e] + KEY_BLOCK - 1) // KEY_BLOCK for e in range(SPANS)]
    for c in range(SPANS):
        tiles = (meta[SPANS + c] + per_tile - 1) // per_tile
        seen = [jnp.where(meta[e] <= meta[c], blocks[e], 0) for e in range(SPANS)]

        def tile_items(t, at, c=c, seen=seen):
            start = at
            for e in range(SPANS):

                def block_item(b, at, e=e):
                    flag = jnp.where(at == start, 1, 0)
                    items[at] = item(c * span_tiles + t, e * span_blocks + b, c, flag)
                    return at + 1

                at = lax.fori_loop(0, seen[e], block_item, at)
            items[at - 1] = items[at - 1] + (2 << 20)
            return at

        at = lax.fori_loop(0, tiles, tile_items, at)
    for extra in range(4 * GROUP):
        items[at + extra] = idle
    items[ITEMS - 1] = at

    per_load = QUERY_TILE // (3 * piece)

    def gather_tile(t, carry):
        rows = []
        for n in range(per_load):
            for k in range(3):
                source = (t * per_load + n) * SPANS + (member + 1 + k) % SPANS
                rows.append(incoming_ref[source].astype(jnp.float32)[skipped:])
        here = pl.ds(pl.multiple_of(t * QUERY_TILE, 16), QUERY_TILE)
        queries[here, :] = jnp.concatenate(rows, axis=0).astype(queries.dtype)
        return carry

    lax.fori_loop(0, SPANS * span_tiles, gather_tile, 0)


def prepare(incoming, meta, tokens):
    smem, vmem = pl.BlockSpec(memory_space=pltpu.SMEM), pl.BlockSpec(memory_space=pltpu.VMEM)
    return pl.pallas_call(
        prepare_kernel,
        out_shape=(
            jax.ShapeDtypeStruct((tokens, HD), incoming.dtype),
            jax.ShapeDtypeStruct((ITEMS,), jnp.int32),
        ),
        in_specs=[smem, vmem],
        out_specs=(vmem, smem),
        compiler_params=pltpu.CompilerParams(vmem_limit_bytes=VMEM_BYTES),
        name="prepare",
    )(meta, incoming)


def attend_kernel(
    meta, gates, items, first_ref, second_ref, queries, o_ref,
    keys, values, scores, highs, weights, scales, acc, top, results, sems,
):
    chunks, piece = o_ref.shape[0], o_ref.shape[1]
    tokens = first_ref.shape[0] // SPANS
    all_tiles = tokens // QUERY_TILE
    core, member = meta[2 * SPANS], meta[2 * SPANS + 1]
    scale = math.log2(math.e) / math.sqrt(HD)

    def loads(key_src, value_src):
        return (
            pltpu.make_async_copy(key_src, keys, sems.at[0]),
            pltpu.make_async_copy(value_src, values.at[:, pl.ds(0, HD)], sems.at[1]),
        )

    @pl.when(core == 0)
    def _():
        for copy in loads(first_ref, second_ref):
            copy.start()

    @pl.when(core != 0)
    def _():
        for copy in loads(second_ref, first_ref):
            copy.start()

    values[:, HD:] = jnp.ones((values.shape[0], HD), values.dtype)
    for copy in loads(first_ref, second_ref):
        copy.wait()

    for e in range(SPANS):
        count = meta[SPANS + e]
        ends = (count + KEY_BLOCK - 1) // KEY_BLOCK * (KEY_BLOCK // EDGE_ROWS)
        first_key = keys[e * tokens : e * tokens + 16, :].astype(jnp.float32)[0:1, :]

        def edge(s, carry, e=e, count=count, first_key=first_key):
            rows = pl.ds(pl.multiple_of(e * tokens + s * EDGE_ROWS, EDGE_ROWS), EDGE_ROWS)
            left = count - s * EDGE_ROWS
            valid = lax.broadcasted_iota(jnp.int32, (EDGE_ROWS, HD), 0) < left
            block = keys[rows, :].astype(jnp.float32)
            keys[rows, :] = jnp.where(valid, block, first_key).astype(keys.dtype)
            for side in range(2):
                columns = slice(side * HD, (side + 1) * HD)
                mixed = values[rows, columns].astype(jnp.float32)
                values[rows, columns] = jnp.where(valid, mixed, 0.0).astype(values.dtype)
            return carry

        lax.fori_loop(count // EDGE_ROWS, ends, edge, 0)

    def key_rows(i):
        return pl.ds(pl.multiple_of((items[i] >> 8 & 255) * KEY_BLOCK, KEY_BLOCK), KEY_BLOCK)

    def parts_of(x):
        return [x[:, n * HD : (n + 1) * HD] for n in range(KEY_BLOCK // HD)]

    def score(i, at):
        tile = jnp.minimum(items[i] & 255, all_tiles - 1)
        q = queries[pl.ds(pl.multiple_of(tile * QUERY_TILE, 16), QUERY_TILE), :]
        x = lax.dot_general(
            q, keys[key_rows(i), :], (((1,), (1,)), ((), ())), preferred_element_type=jnp.float32
        )
        scores[at][...] = x
        highs[at][...] = functools.reduce(jnp.maximum, parts_of(x))

    def weigh(i, at):
        old = jnp.where((items[i] >> 20) & 1 == 1, -1e30, top[...])
        new = jnp.maximum(old, jnp.max(highs[at][...], axis=1, keepdims=True) * scale)
        top[...] = new
        scales[at][...] = jnp.exp2(old - new)
        for n, part in enumerate(parts_of(scores[at])):
            weight = jnp.exp2(part * scale - new)
            weights[at][:, n * HD : (n + 1) * HD] = weight.astype(jnp.bfloat16)

    def mix(i, at):
        mixed = jnp.dot(weights[at][...], values[key_rows(i), :], preferred_element_type=jnp.float32)
        factor = scales[at][...]
        sums = acc[:, :HD] * factor + mixed[:, :HD]
        totals = acc[:, HD:] * factor + mixed[:, HD:]
        acc[:, :HD] = sums
        acc[:, HD:] = totals
        rows = pl.ds(pl.multiple_of((items[i] & 255) * QUERY_TILE, 16), QUERY_TILE)
        results[rows, :] = sums * (gates[items[i] >> 16 & 3] / totals)

    acc[...] = jnp.ones(acc.shape, acc.dtype)
    top[...] = jnp.zeros(top.shape, top.dtype)
    for g in range(GROUP):
        weights[g][...] = jnp.ones(weights[g].shape, weights[g].dtype)
        scales[g][...] = jnp.zeros(scales[g].shape, scales[g].dtype)
        score(GROUP + g, GROUP + g)

    def two_steps(j, carry):
        for half in range(2):
            here, there = (half + 1) % 2 * GROUP, half * GROUP
            first = (2 * j + half) * GROUP
            for g in range(GROUP):
                score(first + 2 * GROUP + g, there + g)
            for g in range(GROUP):
                weigh(first + GROUP + g, here + g)
            for g in range(GROUP):
                mix(first + g, there + g)
        return carry

    lax.fori_loop(0, (items[ITEMS - 1] + 2 * GROUP - 1) // (2 * GROUP), two_steps, 0)

    def hand_back(t, carry):
        for k in range(3):
            rows = pl.ds(pl.multiple_of((t * 3 + k) * piece, 8), piece)
            o_ref[t * SPANS + (member + 1 + k) % SPANS] = results[rows, :].astype(o_ref.dtype)
        return carry

    lax.fori_loop(0, chunks // SPANS, hand_back, 0)


def attend(first, second, incoming, meta, gates):
    chunks = incoming.shape[0]
    piece = incoming.shape[1] - first.shape[0] // chunks
    tokens = first.shape[0] // SPANS
    queries, items = prepare(incoming, meta, tokens)
    smem, anywhere = pl.BlockSpec(memory_space=pltpu.SMEM), pl.BlockSpec(memory_space=pl.ANY)
    vmem = pl.BlockSpec(memory_space=pltpu.VMEM)
    tile, strip = (QUERY_TILE, KEY_BLOCK), (QUERY_TILE, HD)
    return pl.pallas_call(
        attend_kernel,
        out_shape=jax.ShapeDtypeStruct((chunks, piece, HD), first.dtype),
        in_specs=[smem, smem, smem, anywhere, anywhere, vmem],
        out_specs=vmem,
        scratch_shapes=[
            pltpu.VMEM(first.shape, first.dtype),
            pltpu.VMEM((first.shape[0], 2 * HD), first.dtype),
            [pltpu.VMEM(tile, jnp.float32)] * (2 * GROUP),
            [pltpu.VMEM(strip, jnp.float32)] * (2 * GROUP),
            [pltpu.VMEM(tile, jnp.bfloat16)] * (2 * GROUP),
            [pltpu.VMEM(strip, jnp.float32)] * (2 * GROUP),
            pltpu.VMEM((QUERY_TILE, 2 * HD), jnp.float32),
            pltpu.VMEM(strip, jnp.float32),
            pltpu.VMEM((tokens + QUERY_TILE, HD), jnp.float32),
            pltpu.SemaphoreType.DMA((2,)),
        ],
        compiler_params=pltpu.CompilerParams(vmem_limit_bytes=VMEM_BYTES),
        name="attend",
    )(meta, gates, items, first, second, queries)


def turned(x, axis, start, length):
    return lax.dynamic_slice_in_dim(jnp.concatenate([x, x], axis=axis), start, length, axis=axis)


def shards(queries, key_rows, value_rows, noise_steps, span_order, token_counts):
    both = ("span", "ctx")
    tok = queries.shape[1]
    piece = tok // 3
    ctx_size = lax.axis_size("ctx")
    me = lax.axis_index("span")
    place = lax.axis_index("ctx")
    turn = place % SPANS
    core = me % 2

    outgoing = pack(turn[None], queries[0], key_rows[0], value_rows[0])
    outgoing = outgoing.reshape(SPANS * HEADS, tok + piece, HD)
    incoming = lax.all_to_all(outgoing, both, split_axis=0, concat_axis=0, tiled=True)

    first = incoming[:, :tok].reshape(SPANS * ctx_size * tok, HD)
    second = lax.ppermute(first, "span", [(0, 1), (1, 0), (2, 3), (3, 2)])
    gates = head_gates(noise_steps, place)
    meta = jnp.concatenate([span_order, token_counts, core[None], me[None]]).astype(jnp.int32)
    out = attend(first, second, incoming, meta, gates)

    back = lax.all_to_all(out, both, split_axis=0, concat_axis=0, tiled=True)
    back = turned(back.reshape(SPANS, HEADS, piece, HD), 0, turn + 1, 3)
    back = back.transpose(0, 2, 1, 3).reshape(tok, HEADS * HD)
    token = place * tok + jnp.arange(tok)
    back = jnp.where((token < token_counts[me])[:, None], back, jnp.zeros((), back.dtype))
    return back[None]


def solution(mesh):
    tokens = P("span", "ctx", None)
    return jax.shard_map(
        shards,
        mesh=mesh,
        in_specs=(tokens, tokens, tokens, P(), P(), P()),
        out_specs=tokens,
        check_vma=False,
    )
```

```python
import functools
import math

import jax
import jax.numpy as jnp
from jax import lax
from jax.experimental import pallas as pl
from jax.experimental.pallas import tpu as pltpu
from jax.sharding import PartitionSpec as P

HEADS = 32
HD = 128
SPANS = 4
KEY_BLOCK = 768
EDGE_ROWS = 128
QUERY_TILE = 144
GROUP = 4
PACK_HEADS = 8
ITEMS = 512
ATTEND_VMEM = 24 * 1024 * 1024
PREPARE_VMEM = 8 * 1024 * 1024


def head_gates(noise_steps, head):
    freq = jnp.exp(-math.log(10000.0) * head.astype(jnp.float32) / HEADS)
    return 1.0 + 0.5 * jnp.sin(noise_steps.astype(jnp.float32) * freq)


def pack_kernel(turn_ref, q_hbm, k_hbm, v_hbm, packed, given, in_sems):
    tok = q_hbm.shape[0]
    piece = tok // 3
    turn = turn_ref[0]
    steps = HEADS // PACK_HEADS

    def arriving(n):
        columns = pl.ds(n * PACK_HEADS * HD, PACK_HEADS * HD)
        return [
            pltpu.make_async_copy(ref.at[:, columns], given.at[side, :, columns], in_sems.at[side, n])
            for side, ref in enumerate((k_hbm, v_hbm, q_hbm))
        ]

    for n in range(steps):
        for copy in arriving(n):
            copy.start()
    for n in range(steps):
        for copy in arriving(n):
            copy.wait()
        for head in range(n * PACK_HEADS, (n + 1) * PACK_HEADS):
            columns = slice(head * HD, (head + 1) * HD)
            sides = [given[side, :, columns].astype(jnp.float32) for side in range(3)]
            pieces = [sides[2][m * piece : (m + 1) * piece] for m in range(3)]
            for member in range(SPANS):
                which = (member + SPANS - 1 - turn) % SPANS
                chosen = jnp.where(
                    which == 0, pieces[0], jnp.where(which == 1, pieces[1], pieces[2])
                )
                chunk = jnp.concatenate([sides[member % 2], chosen], axis=0)
                packed[member, head] = chunk.astype(packed.dtype)


def pack(turn, q, k, v):
    tok = q.shape[0]
    hbm = pl.BlockSpec(memory_space=pltpu.HBM)
    q, k, v = (pltpu.with_memory_space_constraint(x, pltpu.HBM) for x in (q, k, v))
    return pl.pallas_call(
        pack_kernel,
        out_shape=pltpu.VMEM((SPANS, HEADS, tok + tok // 3, HD), q.dtype),
        in_specs=[pl.BlockSpec(memory_space=pltpu.SMEM), hbm, hbm, hbm],
        out_specs=pl.BlockSpec(memory_space=pltpu.VMEM),
        scratch_shapes=[
            pltpu.VMEM((3,) + q.shape, q.dtype),
            pltpu.SemaphoreType.DMA((3, HEADS // PACK_HEADS)),
        ],
        compiler_params=pltpu.CompilerParams(vmem_limit_bytes=PREPARE_VMEM),
        name="pack",
    )(turn, q, k, v)


def prepare_kernel(meta, incoming_ref, queries, items):
    tokens = queries.shape[0]
    piece = tokens // (3 * incoming_ref.shape[0] // SPANS)
    skipped = incoming_ref.shape[1] - piece
    span_tiles = tokens // SPANS // QUERY_TILE
    member = meta[2 * SPANS + 1]

    def item(tile, block, span, flag):
        return tile + (block << 8) + (span << 16) + (flag << 20)

    idle = item(SPANS * span_tiles, 0, 0, 1)
    at = jnp.int32(GROUP)
    for extra in range(GROUP):
        items[extra] = idle
    per_tile = SPANS * QUERY_TILE
    span_blocks = tokens // KEY_BLOCK
    blocks = [(meta[SPANS + e] + KEY_BLOCK - 1) // KEY_BLOCK for e in range(SPANS)]
    for c in range(SPANS):
        tiles = (meta[SPANS + c] + per_tile - 1) // per_tile
        seen = [jnp.where(meta[e] <= meta[c], blocks[e], 0) for e in range(SPANS)]

        def tile_items(t, at, c=c, seen=seen):
            start = at
            for e in range(SPANS):

                def block_item(b, at, e=e):
                    flag = jnp.where(at == start, 1, 0)
                    items[at] = item(c * span_tiles + t, e * span_blocks + b, c, flag)
                    return at + 1

                at = lax.fori_loop(0, seen[e], block_item, at)
            items[at - 1] = items[at - 1] + (2 << 20)
            return at

        at = lax.fori_loop(0, tiles, tile_items, at)
    for extra in range(4 * GROUP):
        items[at + extra] = idle
    items[ITEMS - 1] = at

    per_load = QUERY_TILE // (3 * piece)

    def gather_tile(t, carry):
        rows = []
        for n in range(per_load):
            for k in range(3):
                source = (t * per_load + n) * SPANS + (member + 1 + k) % SPANS
                rows.append(incoming_ref[source].astype(jnp.float32)[skipped:])
        here = pl.ds(pl.multiple_of(t * QUERY_TILE, 16), QUERY_TILE)
        queries[here, :] = jnp.concatenate(rows, axis=0).astype(queries.dtype)
        return carry

    lax.fori_loop(0, SPANS * span_tiles, gather_tile, 0)


def prepare(incoming, meta, tokens):
    smem, vmem = pl.BlockSpec(memory_space=pltpu.SMEM), pl.BlockSpec(memory_space=pltpu.VMEM)
    return pl.pallas_call(
        prepare_kernel,
        out_shape=(
            pltpu.VMEM((tokens, HD), incoming.dtype),
            jax.ShapeDtypeStruct((ITEMS,), jnp.int32),
        ),
        in_specs=[smem, vmem],
        out_specs=(vmem, smem),
        compiler_params=pltpu.CompilerParams(vmem_limit_bytes=PREPARE_VMEM),
        name="prepare",
    )(meta, incoming)


def attend_kernel(
    meta, gates, items, first_ref, second_ref, queries, o_ref,
    keys, values, scores, highs, weights, scales, acc, top, results, sems,
):
    chunks, piece = o_ref.shape[0], o_ref.shape[1]
    tokens = first_ref.shape[0] // SPANS
    all_tiles = tokens // QUERY_TILE
    core, member = meta[2 * SPANS], meta[2 * SPANS + 1]
    scale = math.log2(math.e) / math.sqrt(HD)

    def loads(key_src, value_src, e):
        rows = pl.ds(e * tokens, tokens)
        return (
            pltpu.make_async_copy(key_src.at[rows], keys.at[rows], sems.at[0, e]),
            pltpu.make_async_copy(
                value_src.at[rows], values.at[rows, pl.ds(0, HD)], sems.at[1, e]
            ),
        )

    @pl.when(core == 0)
    def _():
        for e in range(SPANS):
            for copy in loads(first_ref, second_ref, e):
                copy.start()

    @pl.when(core != 0)
    def _():
        for e in range(SPANS):
            for copy in loads(second_ref, first_ref, e):
                copy.start()

    values[:, HD:] = jnp.ones((values.shape[0], HD), values.dtype)

    for e in range(SPANS):
        for copy in loads(first_ref, second_ref, e):
            copy.wait()
        count = meta[SPANS + e]
        ends = (count + KEY_BLOCK - 1) // KEY_BLOCK * (KEY_BLOCK // EDGE_ROWS)
        first_key = keys[e * tokens : e * tokens + 16, :].astype(jnp.float32)[0:1, :]

        def edge(s, carry, e=e, count=count, first_key=first_key):
            rows = pl.ds(pl.multiple_of(e * tokens + s * EDGE_ROWS, EDGE_ROWS), EDGE_ROWS)
            left = count - s * EDGE_ROWS
            valid = lax.broadcasted_iota(jnp.int32, (EDGE_ROWS, HD), 0) < left
            block = keys[rows, :].astype(jnp.float32)
            keys[rows, :] = jnp.where(valid, block, first_key).astype(keys.dtype)
            for side in range(2):
                columns = slice(side * HD, (side + 1) * HD)
                mixed = values[rows, columns].astype(jnp.float32)
                values[rows, columns] = jnp.where(valid, mixed, 0.0).astype(values.dtype)
            return carry

        lax.fori_loop(count // EDGE_ROWS, ends, edge, 0)

    def key_rows(i):
        return pl.ds(pl.multiple_of((items[i] >> 8 & 255) * KEY_BLOCK, KEY_BLOCK), KEY_BLOCK)

    def parts_of(x):
        return [x[:, n * HD : (n + 1) * HD] for n in range(KEY_BLOCK // HD)]

    def score(i, at):
        tile = jnp.minimum(items[i] & 255, all_tiles - 1)
        q = queries[pl.ds(pl.multiple_of(tile * QUERY_TILE, 16), QUERY_TILE), :]
        x = lax.dot_general(
            q, keys[key_rows(i), :], (((1,), (1,)), ((), ())), preferred_element_type=jnp.float32
        )
        scores[at][...] = x
        highs[at][...] = functools.reduce(jnp.maximum, parts_of(x))

    def weigh(i, at):
        old = jnp.where((items[i] >> 20) & 1 == 1, -1e30, top[...])
        new = jnp.maximum(old, jnp.max(highs[at][...], axis=1, keepdims=True) * scale)
        top[...] = new
        scales[at][...] = jnp.exp2(old - new)
        for n, part in enumerate(parts_of(scores[at])):
            weight = jnp.exp2(part * scale - new)
            weights[at][:, n * HD : (n + 1) * HD] = weight.astype(jnp.bfloat16)

    def mix(i, at):
        mixed = jnp.dot(weights[at][...], values[key_rows(i), :], preferred_element_type=jnp.float32)
        factor = scales[at][...]
        sums = acc[:, :HD] * factor + mixed[:, :HD]
        totals = acc[:, HD:] * factor + mixed[:, HD:]
        acc[:, :HD] = sums
        acc[:, HD:] = totals
        rows = pl.ds(pl.multiple_of((items[i] & 255) * QUERY_TILE, 16), QUERY_TILE)
        results[rows, :] = sums * (gates[items[i] >> 16 & 3] / totals)

    acc[...] = jnp.ones(acc.shape, acc.dtype)
    top[...] = jnp.zeros(top.shape, top.dtype)
    for g in range(GROUP):
        weights[g][...] = jnp.ones(weights[g].shape, weights[g].dtype)
        scales[g][...] = jnp.zeros(scales[g].shape, scales[g].dtype)
        score(GROUP + g, GROUP + g)

    def two_steps(j, carry):
        for half in range(2):
            here, there = (half + 1) % 2 * GROUP, half * GROUP
            first = (2 * j + half) * GROUP
            for g in range(GROUP):
                score(first + 2 * GROUP + g, there + g)
            for g in range(GROUP):
                weigh(first + GROUP + g, here + g)
            for g in range(GROUP):
                mix(first + g, there + g)
        return carry

    lax.fori_loop(0, (items[ITEMS - 1] + 2 * GROUP - 1) // (2 * GROUP), two_steps, 0)

    def hand_back(t, carry):
        for k in range(3):
            rows = pl.ds(pl.multiple_of((t * 3 + k) * piece, 8), piece)
            o_ref[t * SPANS + (member + 1 + k) % SPANS] = results[rows, :].astype(o_ref.dtype)
        return carry

    lax.fori_loop(0, chunks // SPANS, hand_back, 0)


def attend(first, second, incoming, meta, gates):
    chunks = incoming.shape[0]
    piece = incoming.shape[1] - first.shape[0] // chunks
    tokens = first.shape[0] // SPANS
    queries, items = prepare(incoming, meta, tokens)
    first = pltpu.with_memory_space_constraint(first, pltpu.VMEM)
    second = pltpu.with_memory_space_constraint(second, pltpu.VMEM)
    smem, anywhere = pl.BlockSpec(memory_space=pltpu.SMEM), pl.BlockSpec(memory_space=pl.ANY)
    vmem = pl.BlockSpec(memory_space=pltpu.VMEM)
    tile, strip = (QUERY_TILE, KEY_BLOCK), (QUERY_TILE, HD)
    return pl.pallas_call(
        attend_kernel,
        out_shape=pltpu.VMEM((chunks, piece, HD), first.dtype),
        in_specs=[smem, smem, smem, anywhere, anywhere, vmem],
        out_specs=vmem,
        scratch_shapes=[
            pltpu.VMEM(first.shape, first.dtype),
            pltpu.VMEM((first.shape[0], 2 * HD), first.dtype),
            [pltpu.VMEM(tile, jnp.float32)] * (2 * GROUP),
            [pltpu.VMEM(strip, jnp.float32)] * (2 * GROUP),
            [pltpu.VMEM(tile, jnp.bfloat16)] * (2 * GROUP),
            [pltpu.VMEM(strip, jnp.float32)] * (2 * GROUP),
            pltpu.VMEM((QUERY_TILE, 2 * HD), jnp.float32),
            pltpu.VMEM(strip, jnp.float32),
            pltpu.VMEM((tokens + QUERY_TILE, HD), jnp.float32),
            pltpu.SemaphoreType.DMA((2, SPANS)),
        ],
        compiler_params=pltpu.CompilerParams(vmem_limit_bytes=ATTEND_VMEM),
        name="attend",
    )(meta, gates, items, first, second, queries)


def turned(x, axis, start, length):
    return lax.dynamic_slice_in_dim(jnp.concatenate([x, x], axis=axis), start, length, axis=axis)


def shards(queries, key_rows, value_rows, noise_steps, span_order, token_counts):
    both = ("span", "ctx")
    tok = queries.shape[1]
    piece = tok // 3
    ctx_size = lax.axis_size("ctx")
    me = lax.axis_index("span")
    place = lax.axis_index("ctx")
    turn = place % SPANS
    core = me % 2

    outgoing = pack(turn[None], queries[0], key_rows[0], value_rows[0])
    outgoing = outgoing.reshape(SPANS * HEADS, tok + piece, HD)
    incoming = lax.all_to_all(outgoing, both, split_axis=0, concat_axis=0, tiled=True)

    first = incoming[:, :tok].reshape(SPANS * ctx_size * tok, HD)
    second = lax.ppermute(first, "span", [(0, 1), (1, 0), (2, 3), (3, 2)])
    gates = head_gates(noise_steps, place)
    meta = jnp.concatenate([span_order, token_counts, core[None], me[None]]).astype(jnp.int32)
    out = attend(first, second, incoming, meta, gates)

    back = lax.all_to_all(out, both, split_axis=0, concat_axis=0, tiled=True)
    back = turned(back.reshape(SPANS, HEADS, piece, HD), 0, turn + 1, 3)
    back = back.transpose(0, 2, 1, 3).reshape(tok, HEADS * HD)
    token = place * tok + jnp.arange(tok)
    back = jnp.where((token < token_counts[me])[:, None], back, jnp.zeros((), back.dtype))
    return back[None]


def solution(mesh):
    tokens = P("span", "ctx", None)
    return jax.shard_map(
        shards,
        mesh=mesh,
        in_specs=(tokens, tokens, tokens, P(), P(), P()),
        out_specs=tokens,
        check_vma=False,
    )
```

```python
import functools
import math

import jax
import jax.numpy as jnp
from jax import lax
from jax.experimental import pallas as pl
from jax.experimental.pallas import tpu as pltpu
from jax.sharding import PartitionSpec as P

HEADS = 32
HD = 128
SPANS = 4
KEY_BLOCK = 768
EDGE_ROWS = 128
QUERY_TILE = 144
GROUP = 6
PACK_HEADS = 8
ITEMS = 512
ATTEND_VMEM = 28 * 1024 * 1024
PREPARE_VMEM = 8 * 1024 * 1024


def head_gates(noise_steps, head):
    freq = jnp.exp(-math.log(10000.0) * head.astype(jnp.float32) / HEADS)
    return 1.0 + 0.5 * jnp.sin(noise_steps.astype(jnp.float32) * freq)


def pack_kernel(turn_ref, q_hbm, k_hbm, v_hbm, packed, given, in_sems):
    tok = q_hbm.shape[0]
    piece = tok // 3
    turn = turn_ref[0]
    steps = HEADS // PACK_HEADS

    def arriving(n):
        columns = pl.ds(n * PACK_HEADS * HD, PACK_HEADS * HD)
        return [
            pltpu.make_async_copy(ref.at[:, columns], given.at[side, :, columns], in_sems.at[side, n])
            for side, ref in enumerate((k_hbm, v_hbm, q_hbm))
        ]

    for n in range(steps):
        for copy in arriving(n):
            copy.start()
    for n in range(steps):
        for copy in arriving(n):
            copy.wait()
        for head in range(n * PACK_HEADS, (n + 1) * PACK_HEADS):
            columns = slice(head * HD, (head + 1) * HD)
            sides = [given[side, :, columns].astype(jnp.float32) for side in range(3)]
            pieces = [sides[2][m * piece : (m + 1) * piece] for m in range(3)]
            for member in range(SPANS):
                which = (member + SPANS - 1 - turn) % SPANS
                chosen = jnp.where(
                    which == 0, pieces[0], jnp.where(which == 1, pieces[1], pieces[2])
                )
                chunk = jnp.concatenate([sides[member % 2], chosen], axis=0)
                packed[member, head] = chunk.astype(packed.dtype)


def pack(turn, q, k, v):
    tok = q.shape[0]
    hbm = pl.BlockSpec(memory_space=pltpu.HBM)
    q, k, v = (pltpu.with_memory_space_constraint(x, pltpu.HBM) for x in (q, k, v))
    return pl.pallas_call(
        pack_kernel,
        out_shape=pltpu.VMEM((SPANS, HEADS, tok + tok // 3, HD), q.dtype),
        in_specs=[pl.BlockSpec(memory_space=pltpu.SMEM), hbm, hbm, hbm],
        out_specs=pl.BlockSpec(memory_space=pltpu.VMEM),
        scratch_shapes=[
            pltpu.VMEM((3,) + q.shape, q.dtype),
            pltpu.SemaphoreType.DMA((3, HEADS // PACK_HEADS)),
        ],
        compiler_params=pltpu.CompilerParams(vmem_limit_bytes=PREPARE_VMEM),
        name="pack",
    )(turn, q, k, v)


def prepare_kernel(meta, incoming_ref, queries, items):
    tokens = queries.shape[0]
    piece = tokens // (3 * incoming_ref.shape[0] // SPANS)
    skipped = incoming_ref.shape[1] - piece
    span_tiles = tokens // SPANS // QUERY_TILE
    member = meta[2 * SPANS + 1]

    def item(tile, block, span, flag):
        return tile + (block << 8) + (span << 16) + (flag << 20)

    idle = item(SPANS * span_tiles, 0, 0, 1)
    at = jnp.int32(0)
    per_tile = SPANS * QUERY_TILE
    span_blocks = tokens // KEY_BLOCK
    blocks = [(meta[SPANS + e] + KEY_BLOCK - 1) // KEY_BLOCK for e in range(SPANS)]
    for c in range(SPANS):
        tiles = (meta[SPANS + c] + per_tile - 1) // per_tile
        seen = [jnp.where(meta[e] <= meta[c], blocks[e], 0) for e in range(SPANS)]

        def tile_items(t, at, c=c, seen=seen):
            start = at
            for e in range(SPANS):

                def block_item(b, at, e=e):
                    flag = jnp.where(at == start, 1, 0)
                    items[at] = item(c * span_tiles + t, e * span_blocks + b, c, flag)
                    return at + 1

                at = lax.fori_loop(0, seen[e], block_item, at)
            items[at - 1] = items[at - 1] + (2 << 20)
            return at

        at = lax.fori_loop(0, tiles, tile_items, at)
    for extra in range(4 * GROUP):
        items[at + extra] = idle
    items[ITEMS - 1] = at

    per_load = QUERY_TILE // (3 * piece)

    def gather_tile(t, carry):
        rows = []
        for n in range(per_load):
            for k in range(3):
                source = (t * per_load + n) * SPANS + (member + 1 + k) % SPANS
                rows.append(incoming_ref[source].astype(jnp.float32)[skipped:])
        here = pl.ds(pl.multiple_of(t * QUERY_TILE, 16), QUERY_TILE)
        queries[here, :] = jnp.concatenate(rows, axis=0).astype(queries.dtype)
        return carry

    lax.fori_loop(0, SPANS * span_tiles, gather_tile, 0)


def prepare(incoming, meta, tokens):
    smem, vmem = pl.BlockSpec(memory_space=pltpu.SMEM), pl.BlockSpec(memory_space=pltpu.VMEM)
    return pl.pallas_call(
        prepare_kernel,
        out_shape=(
            pltpu.VMEM((tokens, HD), incoming.dtype),
            jax.ShapeDtypeStruct((ITEMS,), jnp.int32),
        ),
        in_specs=[smem, vmem],
        out_specs=(vmem, smem),
        compiler_params=pltpu.CompilerParams(vmem_limit_bytes=PREPARE_VMEM),
        name="prepare",
    )(meta, incoming)


def attend_kernel(
    meta, gates, items, first_ref, second_ref, queries, o_ref,
    keys, values, scores, highs, weights, scales, acc, top, results, sems,
):
    chunks, piece = o_ref.shape[0], o_ref.shape[1]
    tokens = first_ref.shape[0] // SPANS
    all_tiles = tokens // QUERY_TILE
    core, member = meta[2 * SPANS], meta[2 * SPANS + 1]
    scale = math.log2(math.e) / math.sqrt(HD)

    def loads(key_src, value_src, e):
        rows = pl.ds(e * tokens, tokens)
        return (
            pltpu.make_async_copy(key_src.at[rows], keys.at[rows], sems.at[0, e]),
            pltpu.make_async_copy(
                value_src.at[rows], values.at[rows, pl.ds(0, HD)], sems.at[1, e]
            ),
        )

    @pl.when(core == 0)
    def _():
        for e in range(SPANS):
            for copy in loads(first_ref, second_ref, e):
                copy.start()

    @pl.when(core != 0)
    def _():
        for e in range(SPANS):
            for copy in loads(second_ref, first_ref, e):
                copy.start()

    values[:, HD:] = jnp.ones((values.shape[0], HD), values.dtype)

    for e in range(SPANS):
        for copy in loads(first_ref, second_ref, e):
            copy.wait()
        count = meta[SPANS + e]
        ends = (count + KEY_BLOCK - 1) // KEY_BLOCK * (KEY_BLOCK // EDGE_ROWS)
        first_key = keys[e * tokens : e * tokens + 16, :].astype(jnp.float32)[0:1, :]

        def edge(s, carry, e=e, count=count, first_key=first_key):
            rows = pl.ds(pl.multiple_of(e * tokens + s * EDGE_ROWS, EDGE_ROWS), EDGE_ROWS)
            left = count - s * EDGE_ROWS
            valid = lax.broadcasted_iota(jnp.int32, (EDGE_ROWS, HD), 0) < left
            block = keys[rows, :].astype(jnp.float32)
            keys[rows, :] = jnp.where(valid, block, first_key).astype(keys.dtype)
            for side in range(2):
                columns = slice(side * HD, (side + 1) * HD)
                mixed = values[rows, columns].astype(jnp.float32)
                values[rows, columns] = jnp.where(valid, mixed, 0.0).astype(values.dtype)
            return carry

        lax.fori_loop(count // EDGE_ROWS, ends, edge, 0)

    def key_rows(i):
        return pl.ds(pl.multiple_of((items[i] >> 8 & 255) * KEY_BLOCK, KEY_BLOCK), KEY_BLOCK)

    def parts_of(x):
        return [x[:, n * HD : (n + 1) * HD] for n in range(KEY_BLOCK // HD)]

    def score(i, at):
        tile = jnp.minimum(items[i] & 255, all_tiles - 1)
        q = queries[pl.ds(pl.multiple_of(tile * QUERY_TILE, 16), QUERY_TILE), :]
        x = lax.dot_general(
            q, keys[key_rows(i), :], (((1,), (1,)), ((), ())), preferred_element_type=jnp.float32
        )
        scores[at][...] = x
        highs[at][...] = functools.reduce(jnp.maximum, parts_of(x))

    def weigh(i, at):
        old = jnp.where((items[i] >> 20) & 1 == 1, -1e30, top[...])
        new = jnp.maximum(old, jnp.max(highs[at][...], axis=1, keepdims=True) * scale)
        top[...] = new
        scales[at][...] = jnp.exp2(old - new)
        for n, part in enumerate(parts_of(scores[at])):
            weight = jnp.exp2(part * scale - new)
            weights[at][:, n * HD : (n + 1) * HD] = weight.astype(jnp.bfloat16)

    def mix(i, at):
        mixed = jnp.dot(weights[at][...], values[key_rows(i), :], preferred_element_type=jnp.float32)
        factor = scales[at][...]
        sums = acc[:, :HD] * factor + mixed[:, :HD]
        totals = acc[:, HD:] * factor + mixed[:, HD:]
        acc[:, :HD] = sums
        acc[:, HD:] = totals
        rows = pl.ds(pl.multiple_of((items[i] & 255) * QUERY_TILE, 16), QUERY_TILE)
        results[rows, :] = sums * (gates[items[i] >> 16 & 3] / totals)

    acc[...] = jnp.ones(acc.shape, acc.dtype)
    top[...] = jnp.zeros(top.shape, top.dtype)

    def group(step, first, at):
        for g in range(GROUP):
            step(first + g, at + g)

    group(score, 0, 0)
    group(score, GROUP, GROUP)
    group(weigh, 0, 0)

    def two_steps(j, carry):
        first = 2 * j * GROUP
        group(score, first + 2 * GROUP, 0)
        group(weigh, first + GROUP, GROUP)
        group(mix, first, 0)
        group(score, first + 3 * GROUP, GROUP)
        group(weigh, first + 2 * GROUP, 0)
        group(mix, first + GROUP, GROUP)
        return carry

    count = items[ITEMS - 1]
    pairs = count // (2 * GROUP)
    lax.fori_loop(0, pairs, two_steps, 0)
    done = pairs * 2 * GROUP

    @pl.when(done < count)
    def _():
        group(mix, done, 0)

    @pl.when(done + GROUP < count)
    def _():
        group(weigh, done + GROUP, GROUP)
        group(mix, done + GROUP, GROUP)

    def hand_back(t, carry):
        for k in range(3):
            rows = pl.ds(pl.multiple_of((t * 3 + k) * piece, 8), piece)
            o_ref[t * SPANS + (member + 1 + k) % SPANS] = results[rows, :].astype(o_ref.dtype)
        return carry

    lax.fori_loop(0, chunks // SPANS, hand_back, 0, unroll=4)


def attend(first, second, incoming, meta, gates):
    chunks = incoming.shape[0]
    piece = incoming.shape[1] - first.shape[0] // chunks
    tokens = first.shape[0] // SPANS
    queries, items = prepare(incoming, meta, tokens)
    first = pltpu.with_memory_space_constraint(first, pltpu.VMEM)
    second = pltpu.with_memory_space_constraint(second, pltpu.VMEM)
    smem, anywhere = pl.BlockSpec(memory_space=pltpu.SMEM), pl.BlockSpec(memory_space=pl.ANY)
    vmem = pl.BlockSpec(memory_space=pltpu.VMEM)
    tile, strip = (QUERY_TILE, KEY_BLOCK), (QUERY_TILE, HD)
    return pl.pallas_call(
        attend_kernel,
        out_shape=pltpu.VMEM((chunks, piece, HD), first.dtype),
        in_specs=[smem, smem, smem, anywhere, anywhere, vmem],
        out_specs=vmem,
        scratch_shapes=[
            pltpu.VMEM(first.shape, first.dtype),
            pltpu.VMEM((first.shape[0], 2 * HD), first.dtype),
            [pltpu.VMEM(tile, jnp.float32)] * (2 * GROUP),
            [pltpu.VMEM(strip, jnp.float32)] * (2 * GROUP),
            [pltpu.VMEM(tile, jnp.bfloat16)] * (2 * GROUP),
            [pltpu.VMEM(strip, jnp.float32)] * (2 * GROUP),
            pltpu.VMEM((QUERY_TILE, 2 * HD), jnp.float32),
            pltpu.VMEM(strip, jnp.float32),
            pltpu.VMEM((tokens + QUERY_TILE, HD), jnp.float32),
            pltpu.SemaphoreType.DMA((2, SPANS)),
        ],
        compiler_params=pltpu.CompilerParams(vmem_limit_bytes=ATTEND_VMEM),
        name="attend",
    )(meta, gates, items, first, second, queries)


def turned(x, axis, start, length):
    return lax.dynamic_slice_in_dim(jnp.concatenate([x, x], axis=axis), start, length, axis=axis)


def shards(queries, key_rows, value_rows, noise_steps, span_order, token_counts):
    both = ("span", "ctx")
    tok = queries.shape[1]
    piece = tok // 3
    ctx_size = lax.axis_size("ctx")
    me = lax.axis_index("span")
    place = lax.axis_index("ctx")
    turn = place % SPANS
    core = me % 2

    outgoing = pack(turn[None], queries[0], key_rows[0], value_rows[0])
    outgoing = outgoing.reshape(SPANS * HEADS, tok + piece, HD)
    incoming = lax.all_to_all(outgoing, both, split_axis=0, concat_axis=0, tiled=True)

    first = incoming[:, :tok].reshape(SPANS * ctx_size * tok, HD)
    second = lax.ppermute(first, "span", [(0, 1), (1, 0), (2, 3), (3, 2)])
    gates = head_gates(noise_steps, place)
    meta = jnp.concatenate([span_order, token_counts, core[None], me[None]]).astype(jnp.int32)
    out = attend(first, second, incoming, meta, gates)

    back = lax.all_to_all(out, both, split_axis=0, concat_axis=0, tiled=True)
    back = turned(back.reshape(SPANS, HEADS, piece, HD), 0, turn + 1, 3)
    back = back.transpose(0, 2, 1, 3).reshape(tok, HEADS * HD)
    token = place * tok + jnp.arange(tok)
    back = jnp.where((token < token_counts[me])[:, None], back, jnp.zeros((), back.dtype))
    return back[None]


def solution(mesh):
    tokens = P("span", "ctx", None)
    return jax.shard_map(
        shards,
        mesh=mesh,
        in_specs=(tokens, tokens, tokens, P(), P(), P()),
        out_specs=tokens,
        check_vma=False,
    )
```

```python
import functools
import math

import jax
import jax.numpy as jnp
from jax import lax
from jax.experimental import pallas as pl
from jax.experimental.pallas import tpu as pltpu
from jax.sharding import PartitionSpec as P

HEADS = 32
HD = 128
SPANS = 4
KEY_BLOCK = 768
EDGE_ROWS = 128
QUERY_TILE = 144
GROUP = 6
PACK_HEADS = 8
ITEMS = 512
ATTEND_VMEM = 28 * 1024 * 1024
PREPARE_VMEM = 8 * 1024 * 1024


def head_gates(noise_steps, head):
    freq = jnp.exp(-math.log(10000.0) * head.astype(jnp.float32) / HEADS)
    return 1.0 + 0.5 * jnp.sin(noise_steps.astype(jnp.float32) * freq)


def pack_kernel(turn_ref, q_hbm, k_hbm, v_hbm, packed, given, in_sems):
    tok = q_hbm.shape[0]
    piece = tok // 3
    turn = turn_ref[0]
    steps = HEADS // PACK_HEADS

    def arriving(n):
        columns = pl.ds(n * PACK_HEADS * HD, PACK_HEADS * HD)
        return [
            pltpu.make_async_copy(ref.at[:, columns], given.at[side, :, columns], in_sems.at[side, n])
            for side, ref in enumerate((k_hbm, v_hbm, q_hbm))
        ]

    for n in range(steps):
        for copy in arriving(n):
            copy.start()
    for n in range(steps):
        for copy in arriving(n):
            copy.wait()
        for head in range(n * PACK_HEADS, (n + 1) * PACK_HEADS):
            columns = slice(head * HD, (head + 1) * HD)
            sides = [given[side, :, columns].astype(jnp.float32) for side in range(3)]
            pieces = [sides[2][m * piece : (m + 1) * piece] for m in range(3)]
            for member in range(SPANS):
                which = (member + SPANS - 1 - turn) % SPANS
                chosen = jnp.where(
                    which == 0, pieces[0], jnp.where(which == 1, pieces[1], pieces[2])
                )
                chunk = jnp.concatenate([sides[member % 2], chosen], axis=0)
                packed[member, head] = chunk.astype(packed.dtype)


def pack(turn, q, k, v):
    tok = q.shape[0]
    hbm = pl.BlockSpec(memory_space=pltpu.HBM)
    q, k, v = (pltpu.with_memory_space_constraint(x, pltpu.HBM) for x in (q, k, v))
    return pl.pallas_call(
        pack_kernel,
        out_shape=pltpu.VMEM((SPANS, HEADS, tok + tok // 3, HD), q.dtype),
        in_specs=[pl.BlockSpec(memory_space=pltpu.SMEM), hbm, hbm, hbm],
        out_specs=pl.BlockSpec(memory_space=pltpu.VMEM),
        scratch_shapes=[
            pltpu.VMEM((3,) + q.shape, q.dtype),
            pltpu.SemaphoreType.DMA((3, HEADS // PACK_HEADS)),
        ],
        compiler_params=pltpu.CompilerParams(vmem_limit_bytes=PREPARE_VMEM),
        name="pack",
    )(turn, q, k, v)


def prepare_kernel(meta, incoming_ref, queries, items):
    tokens = queries.shape[0]
    piece = tokens // (3 * incoming_ref.shape[0] // SPANS)
    skipped = incoming_ref.shape[1] - piece
    span_tiles = tokens // SPANS // QUERY_TILE
    member = meta[2 * SPANS + 1]

    def item(tile, block, span, flag):
        return tile + (block << 8) + (span << 16) + (flag << 20)

    idle = item(SPANS * span_tiles, 0, 0, 1)
    at = jnp.int32(0)
    per_tile = SPANS * QUERY_TILE
    span_blocks = tokens // KEY_BLOCK
    blocks = [(meta[SPANS + e] + KEY_BLOCK - 1) // KEY_BLOCK for e in range(SPANS)]
    for c in range(SPANS):
        tiles = (meta[SPANS + c] + per_tile - 1) // per_tile
        seen = [jnp.where(meta[e] <= meta[c], blocks[e], 0) for e in range(SPANS)]

        def tile_items(t, at, c=c, seen=seen):
            start = at
            for e in range(SPANS):

                def block_item(b, at, e=e):
                    flag = jnp.where(at == start, 1, 0)
                    items[at] = item(c * span_tiles + t, e * span_blocks + b, c, flag)
                    return at + 1

                at = lax.fori_loop(0, seen[e], block_item, at)
            items[at - 1] = items[at - 1] + (2 << 20)
            return at

        at = lax.fori_loop(0, tiles, tile_items, at)
    for extra in range(4 * GROUP):
        items[at + extra] = idle
    items[ITEMS - 1] = at

    per_load = QUERY_TILE // (3 * piece)

    def gather_tile(t, carry):
        rows = []
        for n in range(per_load):
            for k in range(3):
                source = (t * per_load + n) * SPANS + (member + 1 + k) % SPANS
                rows.append(incoming_ref[source].astype(jnp.float32)[skipped:])
        here = pl.ds(pl.multiple_of(t * QUERY_TILE, 16), QUERY_TILE)
        queries[here, :] = jnp.concatenate(rows, axis=0).astype(queries.dtype)
        return carry

    lax.fori_loop(0, SPANS * span_tiles, gather_tile, 0)


def prepare(incoming, meta, tokens):
    smem, vmem = pl.BlockSpec(memory_space=pltpu.SMEM), pl.BlockSpec(memory_space=pltpu.VMEM)
    return pl.pallas_call(
        prepare_kernel,
        out_shape=(
            pltpu.VMEM((tokens, HD), incoming.dtype),
            jax.ShapeDtypeStruct((ITEMS,), jnp.int32),
        ),
        in_specs=[smem, vmem],
        out_specs=(vmem, smem),
        compiler_params=pltpu.CompilerParams(vmem_limit_bytes=PREPARE_VMEM),
        name="prepare",
    )(meta, incoming)


def attend_kernel(
    meta, gates, items, first_ref, second_ref, queries, o_ref,
    keys, values, scores, highs, weights, scales, acc, top, results, sems,
):
    piece = o_ref.shape[1]
    tokens = first_ref.shape[0] // SPANS
    all_tiles = tokens // QUERY_TILE
    core, member = meta[2 * SPANS], meta[2 * SPANS + 1]
    scale = math.log2(math.e) / math.sqrt(HD)

    def loads(key_src, value_src, e):
        rows = pl.ds(e * tokens, tokens)
        return (
            pltpu.make_async_copy(key_src.at[rows], keys.at[rows], sems.at[0, e]),
            pltpu.make_async_copy(
                value_src.at[rows], values.at[rows, pl.ds(0, HD)], sems.at[1, e]
            ),
        )

    @pl.when(core == 0)
    def _():
        for e in range(SPANS):
            for copy in loads(first_ref, second_ref, e):
                copy.start()

    @pl.when(core != 0)
    def _():
        for e in range(SPANS):
            for copy in loads(second_ref, first_ref, e):
                copy.start()

    values[:, HD:] = jnp.ones((values.shape[0], HD), values.dtype)

    for e in range(SPANS):
        for copy in loads(first_ref, second_ref, e):
            copy.wait()
        count = meta[SPANS + e]
        ends = (count + KEY_BLOCK - 1) // KEY_BLOCK * (KEY_BLOCK // EDGE_ROWS)
        first_key = keys[e * tokens : e * tokens + 16, :].astype(jnp.float32)[0:1, :]

        def edge(s, carry, e=e, count=count, first_key=first_key):
            rows = pl.ds(pl.multiple_of(e * tokens + s * EDGE_ROWS, EDGE_ROWS), EDGE_ROWS)
            left = count - s * EDGE_ROWS
            valid = lax.broadcasted_iota(jnp.int32, (EDGE_ROWS, HD), 0) < left
            block = keys[rows, :].astype(jnp.float32)
            keys[rows, :] = jnp.where(valid, block, first_key).astype(keys.dtype)
            for side in range(2):
                columns = slice(side * HD, (side + 1) * HD)
                mixed = values[rows, columns].astype(jnp.float32)
                values[rows, columns] = jnp.where(valid, mixed, 0.0).astype(values.dtype)
            return carry

        def fill(s, carry, e=e, first_key=first_key):
            rows = pl.ds(pl.multiple_of(e * tokens + s * EDGE_ROWS, EDGE_ROWS), EDGE_ROWS)
            keys[rows, :] = jnp.broadcast_to(first_key, (EDGE_ROWS, HD)).astype(keys.dtype)
            values[rows, :] = jnp.zeros((EDGE_ROWS, 2 * HD), values.dtype)
            return carry

        full = (count + EDGE_ROWS - 1) // EDGE_ROWS
        lax.fori_loop(count // EDGE_ROWS, full, edge, 0)
        lax.fori_loop(full, ends, fill, 0)

    def key_rows(i):
        return pl.ds(pl.multiple_of((items[i] >> 8 & 255) * KEY_BLOCK, KEY_BLOCK), KEY_BLOCK)

    def parts_of(x):
        return [x[:, n * HD : (n + 1) * HD] for n in range(KEY_BLOCK // HD)]

    def score(i, at):
        tile = jnp.minimum(items[i] & 255, all_tiles - 1)
        q = queries[pl.ds(pl.multiple_of(tile * QUERY_TILE, 16), QUERY_TILE), :]
        x = lax.dot_general(
            q, keys[key_rows(i), :], (((1,), (1,)), ((), ())), preferred_element_type=jnp.float32
        )
        scores[at][...] = x
        highs[at][...] = functools.reduce(jnp.maximum, parts_of(x))

    def weigh(i, at):
        old = jnp.where((items[i] >> 20) & 1 == 1, -1e30, top[...])
        new = jnp.maximum(old, jnp.max(highs[at][...], axis=1, keepdims=True) * scale)
        top[...] = new
        scales[at][...] = jnp.exp2(old - new)
        for n, part in enumerate(parts_of(scores[at])):
            weight = jnp.exp2(part * scale - new)
            weights[at][:, n * HD : (n + 1) * HD] = weight.astype(jnp.bfloat16)

    def mix(i, at):
        mixed = jnp.dot(weights[at][...], values[key_rows(i), :], preferred_element_type=jnp.float32)
        factor = scales[at][...]
        sums = acc[:, :HD] * factor + mixed[:, :HD]
        totals = acc[:, HD:] * factor + mixed[:, HD:]
        acc[:, :HD] = sums
        acc[:, HD:] = totals
        rows = pl.ds(pl.multiple_of((items[i] & 255) * QUERY_TILE, 16), QUERY_TILE)
        results[rows, :] = sums * (gates[items[i] >> 16 & 3] / totals)

    acc[...] = jnp.ones(acc.shape, acc.dtype)
    top[...] = jnp.zeros(top.shape, top.dtype)

    def group(step, first, at):
        for g in range(GROUP):
            step(first + g, at + g)

    group(score, 0, 0)
    group(score, GROUP, GROUP)
    group(weigh, 0, 0)

    def two_steps(j, carry):
        first = 2 * j * GROUP
        group(score, first + 2 * GROUP, 0)
        group(weigh, first + GROUP, GROUP)
        group(mix, first, 0)
        group(score, first + 3 * GROUP, GROUP)
        group(weigh, first + 2 * GROUP, 0)
        group(mix, first + GROUP, GROUP)
        return carry

    count = items[ITEMS - 1]
    pairs = count // (2 * GROUP)
    lax.fori_loop(0, pairs, two_steps, 0)
    done = pairs * 2 * GROUP

    @pl.when((done < count) & (done + GROUP >= count))
    def _():
        group(mix, done, 0)

    @pl.when(done + GROUP < count)
    def _():
        group(weigh, done + GROUP, GROUP)
        group(mix, done, 0)
        group(mix, done + GROUP, GROUP)

    per_load = QUERY_TILE // (3 * piece)
    for c in range(SPANS):

        def hand_back(t, carry, c=c):
            for n in range(per_load):
                group_of = (c * all_tiles // SPANS + t) * per_load + n
                for k in range(3):
                    rows = pl.ds(pl.multiple_of((group_of * 3 + k) * piece, 8), piece)
                    source = group_of * SPANS + (member + 1 + k) % SPANS
                    o_ref[source] = results[rows, :].astype(o_ref.dtype)
            return carry

        per_tile = SPANS * QUERY_TILE
        lax.fori_loop(0, (meta[SPANS + c] + per_tile - 1) // per_tile, hand_back, 0)


def attend(first, second, incoming, meta, gates):
    chunks = incoming.shape[0]
    piece = incoming.shape[1] - first.shape[0] // chunks
    tokens = first.shape[0] // SPANS
    queries, items = prepare(incoming, meta, tokens)
    first = pltpu.with_memory_space_constraint(first, pltpu.VMEM)
    second = pltpu.with_memory_space_constraint(second, pltpu.VMEM)
    smem, anywhere = pl.BlockSpec(memory_space=pltpu.SMEM), pl.BlockSpec(memory_space=pl.ANY)
    vmem = pl.BlockSpec(memory_space=pltpu.VMEM)
    tile, strip = (QUERY_TILE, KEY_BLOCK), (QUERY_TILE, HD)
    return pl.pallas_call(
        attend_kernel,
        out_shape=pltpu.VMEM((chunks, piece, HD), first.dtype),
        in_specs=[smem, smem, smem, anywhere, anywhere, vmem],
        out_specs=vmem,
        scratch_shapes=[
            pltpu.VMEM(first.shape, first.dtype),
            pltpu.VMEM((first.shape[0], 2 * HD), first.dtype),
            [pltpu.VMEM(tile, jnp.float32)] * (2 * GROUP),
            [pltpu.VMEM(strip, jnp.float32)] * (2 * GROUP),
            [pltpu.VMEM(tile, jnp.bfloat16)] * (2 * GROUP),
            [pltpu.VMEM(strip, jnp.float32)] * (2 * GROUP),
            pltpu.VMEM((QUERY_TILE, 2 * HD), jnp.float32),
            pltpu.VMEM(strip, jnp.float32),
            pltpu.VMEM((tokens + QUERY_TILE, HD), jnp.float32),
            pltpu.SemaphoreType.DMA((2, SPANS)),
        ],
        compiler_params=pltpu.CompilerParams(vmem_limit_bytes=ATTEND_VMEM),
        name="attend",
    )(meta, gates, items, first, second, queries)


def turned(x, axis, start, length):
    return lax.dynamic_slice_in_dim(jnp.concatenate([x, x], axis=axis), start, length, axis=axis)


def shards(queries, key_rows, value_rows, noise_steps, span_order, token_counts):
    both = ("span", "ctx")
    tok = queries.shape[1]
    piece = tok // 3
    ctx_size = lax.axis_size("ctx")
    me = lax.axis_index("span")
    place = lax.axis_index("ctx")
    turn = place % SPANS
    core = me % 2

    outgoing = pack(turn[None], queries[0], key_rows[0], value_rows[0])
    outgoing = outgoing.reshape(SPANS * HEADS, tok + piece, HD)
    incoming = lax.all_to_all(outgoing, both, split_axis=0, concat_axis=0, tiled=True)

    first = incoming[:, :tok].reshape(SPANS * ctx_size * tok, HD)
    second = lax.ppermute(first, "span", [(0, 1), (1, 0), (2, 3), (3, 2)])
    gates = head_gates(noise_steps, place)
    meta = jnp.concatenate([span_order, token_counts, core[None], me[None]]).astype(jnp.int32)
    out = attend(first, second, incoming, meta, gates)

    back = lax.all_to_all(out, both, split_axis=0, concat_axis=0, tiled=True)
    back = turned(back.reshape(SPANS, HEADS, piece, HD), 0, turn + 1, 3)
    back = back.transpose(0, 2, 1, 3).reshape(tok, HEADS * HD)
    token = place * tok + jnp.arange(tok)
    back = jnp.where((token < token_counts[me])[:, None], back, jnp.zeros((), back.dtype))
    return back[None]


def solution(mesh):
    tokens = P("span", "ctx", None)
    return jax.shard_map(
        shards,
        mesh=mesh,
        in_specs=(tokens, tokens, tokens, P(), P(), P()),
        out_specs=tokens,
        check_vma=False,
    )
```

```python
import functools
import math

import jax
import jax.numpy as jnp
from jax import lax
from jax.experimental import pallas as pl
from jax.experimental.pallas import tpu as pltpu
from jax.sharding import PartitionSpec as P

HEADS = 32
HD = 128
SPANS = 4
KEY_BLOCK = 768
EDGE_ROWS = 128
QUERY_TILE = 144
GROUP = 5
PACK_HEADS = 8
ITEMS = 512
ATTEND_VMEM = 28 * 1024 * 1024
PREPARE_VMEM = 8 * 1024 * 1024


def head_gates(noise_steps, head):
    freq = jnp.exp(-math.log(10000.0) * head.astype(jnp.float32) / HEADS)
    return 1.0 + 0.5 * jnp.sin(noise_steps.astype(jnp.float32) * freq)


def pack_kernel(turn_ref, q_hbm, k_hbm, v_hbm, packed, given, in_sems):
    tok = q_hbm.shape[0]
    piece = tok // 3
    turn = turn_ref[0]
    steps = HEADS // PACK_HEADS

    def arriving(n):
        columns = pl.ds(n * PACK_HEADS * HD, PACK_HEADS * HD)
        return [
            pltpu.make_async_copy(ref.at[:, columns], given.at[side, :, columns], in_sems.at[side, n])
            for side, ref in enumerate((k_hbm, v_hbm, q_hbm))
        ]

    for n in range(steps):
        for copy in arriving(n):
            copy.start()
    for n in range(steps):
        for copy in arriving(n):
            copy.wait()
        for head in range(n * PACK_HEADS, (n + 1) * PACK_HEADS):
            columns = slice(head * HD, (head + 1) * HD)
            sides = [given[side, :, columns].astype(jnp.float32) for side in range(3)]
            pieces = [sides[2][m * piece : (m + 1) * piece] for m in range(3)]
            for member in range(SPANS):
                which = (member + SPANS - 1 - turn) % SPANS
                chosen = jnp.where(
                    which == 0, pieces[0], jnp.where(which == 1, pieces[1], pieces[2])
                )
                chunk = jnp.concatenate([sides[member % 2], chosen], axis=0)
                packed[member, head] = chunk.astype(packed.dtype)


def pack(turn, q, k, v):
    tok = q.shape[0]
    hbm = pl.BlockSpec(memory_space=pltpu.HBM)
    q, k, v = (pltpu.with_memory_space_constraint(x, pltpu.HBM) for x in (q, k, v))
    return pl.pallas_call(
        pack_kernel,
        out_shape=pltpu.VMEM((SPANS, HEADS, tok + tok // 3, HD), q.dtype),
        in_specs=[pl.BlockSpec(memory_space=pltpu.SMEM), hbm, hbm, hbm],
        out_specs=pl.BlockSpec(memory_space=pltpu.VMEM),
        scratch_shapes=[
            pltpu.VMEM((3,) + q.shape, q.dtype),
            pltpu.SemaphoreType.DMA((3, HEADS // PACK_HEADS)),
        ],
        compiler_params=pltpu.CompilerParams(vmem_limit_bytes=PREPARE_VMEM),
        name="pack",
    )(turn, q, k, v)


def prepare_kernel(meta, incoming_ref, queries, items):
    tokens = queries.shape[0]
    piece = tokens // (3 * incoming_ref.shape[0] // SPANS)
    skipped = incoming_ref.shape[1] - piece
    span_tiles = tokens // SPANS // QUERY_TILE
    member = meta[2 * SPANS + 1]

    def item(tile, block, span, flag):
        return tile + (block << 8) + (span << 16) + (flag << 20)

    idle = item(SPANS * span_tiles, 0, 0, 1)
    at = jnp.int32(0)
    per_tile = SPANS * QUERY_TILE
    span_blocks = tokens // KEY_BLOCK
    blocks = [(meta[SPANS + e] + KEY_BLOCK - 1) // KEY_BLOCK for e in range(SPANS)]
    for c in range(SPANS):
        tiles = (meta[SPANS + c] + per_tile - 1) // per_tile
        seen = [jnp.where(meta[e] <= meta[c], blocks[e], 0) for e in range(SPANS)]

        def tile_items(t, at, c=c, seen=seen):
            start = at
            for e in range(SPANS):

                def block_item(b, at, e=e):
                    flag = jnp.where(at == start, 1, 0)
                    items[at] = item(c * span_tiles + t, e * span_blocks + b, c, flag)
                    return at + 1

                at = lax.fori_loop(0, seen[e], block_item, at)
            items[at - 1] = items[at - 1] + (2 << 20)
            return at

        at = lax.fori_loop(0, tiles, tile_items, at)
    for extra in range(4 * GROUP):
        items[at + extra] = idle
    items[ITEMS - 1] = at

    per_load = QUERY_TILE // (3 * piece)

    def gather_tile(t, carry):
        rows = []
        for n in range(per_load):
            for k in range(3):
                source = (t * per_load + n) * SPANS + (member + 1 + k) % SPANS
                rows.append(incoming_ref[source].astype(jnp.float32)[skipped:])
        here = pl.ds(pl.multiple_of(t * QUERY_TILE, 16), QUERY_TILE)
        queries[here, :] = jnp.concatenate(rows, axis=0).astype(queries.dtype)
        return carry

    lax.fori_loop(0, SPANS * span_tiles, gather_tile, 0)


def prepare(incoming, meta, tokens):
    smem, vmem = pl.BlockSpec(memory_space=pltpu.SMEM), pl.BlockSpec(memory_space=pltpu.VMEM)
    return pl.pallas_call(
        prepare_kernel,
        out_shape=(
            pltpu.VMEM((tokens, HD), incoming.dtype),
            jax.ShapeDtypeStruct((ITEMS,), jnp.int32),
        ),
        in_specs=[smem, vmem],
        out_specs=(vmem, smem),
        compiler_params=pltpu.CompilerParams(vmem_limit_bytes=PREPARE_VMEM),
        name="prepare",
    )(meta, incoming)


def attend_kernel(
    meta, gates, items, first_ref, second_ref, queries, o_ref,
    keys, values, scores, highs, weights, scales, acc, top, results, sems,
):
    piece = o_ref.shape[1]
    tokens = first_ref.shape[0] // SPANS
    all_tiles = tokens // QUERY_TILE
    core, member = meta[2 * SPANS], meta[2 * SPANS + 1]
    scale = math.log2(math.e) / math.sqrt(HD)

    def loads(key_src, value_src, e):
        rows = pl.ds(e * tokens, tokens)
        return (
            pltpu.make_async_copy(key_src.at[rows], keys.at[rows], sems.at[0, e]),
            pltpu.make_async_copy(
                value_src.at[rows], values.at[rows, pl.ds(0, HD)], sems.at[1, e]
            ),
        )

    @pl.when(core == 0)
    def _():
        for e in range(SPANS):
            for copy in loads(first_ref, second_ref, e):
                copy.start()

    @pl.when(core != 0)
    def _():
        for e in range(SPANS):
            for copy in loads(second_ref, first_ref, e):
                copy.start()

    values[:, HD:] = jnp.ones((values.shape[0], HD), values.dtype)

    for e in range(SPANS):
        for copy in loads(first_ref, second_ref, e):
            copy.wait()
        count = meta[SPANS + e]
        ends = (count + KEY_BLOCK - 1) // KEY_BLOCK * (KEY_BLOCK // EDGE_ROWS)
        first_key = keys[e * tokens : e * tokens + 16, :].astype(jnp.float32)[0:1, :]

        def edge(s, carry, e=e, count=count, first_key=first_key):
            rows = pl.ds(pl.multiple_of(e * tokens + s * EDGE_ROWS, EDGE_ROWS), EDGE_ROWS)
            left = count - s * EDGE_ROWS
            valid = lax.broadcasted_iota(jnp.int32, (EDGE_ROWS, HD), 0) < left
            block = keys[rows, :].astype(jnp.float32)
            keys[rows, :] = jnp.where(valid, block, first_key).astype(keys.dtype)
            for side in range(2):
                columns = slice(side * HD, (side + 1) * HD)
                mixed = values[rows, columns].astype(jnp.float32)
                values[rows, columns] = jnp.where(valid, mixed, 0.0).astype(values.dtype)
            return carry

        def fill(s, carry, e=e, first_key=first_key):
            rows = pl.ds(pl.multiple_of(e * tokens + s * EDGE_ROWS, EDGE_ROWS), EDGE_ROWS)
            keys[rows, :] = jnp.broadcast_to(first_key, (EDGE_ROWS, HD)).astype(keys.dtype)
            values[rows, :] = jnp.zeros((EDGE_ROWS, 2 * HD), values.dtype)
            return carry

        full = (count + EDGE_ROWS - 1) // EDGE_ROWS
        lax.fori_loop(count // EDGE_ROWS, full, edge, 0)
        lax.fori_loop(full, ends, fill, 0)

    def key_rows(i):
        return pl.ds(pl.multiple_of((items[i] >> 8 & 255) * KEY_BLOCK, KEY_BLOCK), KEY_BLOCK)

    def parts_of(x):
        return [x[:, n * HD : (n + 1) * HD] for n in range(KEY_BLOCK // HD)]

    def score(i, at):
        tile = jnp.minimum(items[i] & 255, all_tiles - 1)
        q = queries[pl.ds(pl.multiple_of(tile * QUERY_TILE, 16), QUERY_TILE), :]
        x = lax.dot_general(
            q, keys[key_rows(i), :], (((1,), (1,)), ((), ())), preferred_element_type=jnp.float32
        )
        scores[at][...] = x
        highs[at][...] = functools.reduce(jnp.maximum, parts_of(x))

    def weigh(i, at):
        old = jnp.where((items[i] >> 20) & 1 == 1, -1e30, top[...])
        new = jnp.maximum(old, jnp.max(highs[at][...], axis=1, keepdims=True) * scale)
        top[...] = new
        scales[at][...] = jnp.exp2(old - new)
        for n, part in enumerate(parts_of(scores[at])):
            weight = jnp.exp2(part * scale - new)
            weights[at][:, n * HD : (n + 1) * HD] = weight.astype(jnp.bfloat16)

    def mix(i, at):
        mixed = jnp.dot(weights[at][...], values[key_rows(i), :], preferred_element_type=jnp.float32)
        factor = scales[at][...]
        sums = acc[:, :HD] * factor + mixed[:, :HD]
        totals = acc[:, HD:] * factor + mixed[:, HD:]
        acc[:, :HD] = sums
        acc[:, HD:] = totals
        rows = pl.ds(pl.multiple_of((items[i] & 255) * QUERY_TILE, 16), QUERY_TILE)
        results[rows, :] = sums * (gates[items[i] >> 16 & 3] / totals)

    acc[...] = jnp.ones(acc.shape, acc.dtype)
    top[...] = jnp.zeros(top.shape, top.dtype)

    def group(step, first, at):
        for g in range(GROUP):
            step(first + g, at + g)

    group(score, 0, 0)
    group(score, GROUP, GROUP)
    group(weigh, 0, 0)

    def two_steps(j, carry):
        first = 2 * j * GROUP
        group(score, first + 2 * GROUP, 0)
        group(weigh, first + GROUP, GROUP)
        group(mix, first, 0)
        group(score, first + 3 * GROUP, GROUP)
        group(weigh, first + 2 * GROUP, 0)
        group(mix, first + GROUP, GROUP)
        return carry

    count = items[ITEMS - 1]
    pairs = count // (2 * GROUP)
    lax.fori_loop(0, pairs, two_steps, 0)
    done = pairs * 2 * GROUP

    @pl.when((done < count) & (done + GROUP >= count))
    def _():
        group(mix, done, 0)

    @pl.when(done + GROUP < count)
    def _():
        group(weigh, done + GROUP, GROUP)
        group(mix, done, 0)
        group(mix, done + GROUP, GROUP)

    per_load = QUERY_TILE // (3 * piece)
    for c in range(SPANS):

        def hand_back(t, carry, c=c):
            for n in range(per_load):
                group_of = (c * all_tiles // SPANS + t) * per_load + n
                for k in range(3):
                    rows = pl.ds(pl.multiple_of((group_of * 3 + k) * piece, 8), piece)
                    source = group_of * SPANS + (member + 1 + k) % SPANS
                    o_ref[source] = results[rows, :].astype(o_ref.dtype)
            return carry

        per_tile = SPANS * QUERY_TILE
        lax.fori_loop(0, (meta[SPANS + c] + per_tile - 1) // per_tile, hand_back, 0)


def attend(first, second, incoming, meta, gates):
    chunks = incoming.shape[0]
    piece = incoming.shape[1] - first.shape[0] // chunks
    tokens = first.shape[0] // SPANS
    queries, items = prepare(incoming, meta, tokens)
    first = pltpu.with_memory_space_constraint(first, pltpu.VMEM)
    second = pltpu.with_memory_space_constraint(second, pltpu.VMEM)
    smem, anywhere = pl.BlockSpec(memory_space=pltpu.SMEM), pl.BlockSpec(memory_space=pl.ANY)
    vmem = pl.BlockSpec(memory_space=pltpu.VMEM)
    tile, strip = (QUERY_TILE, KEY_BLOCK), (QUERY_TILE, HD)
    return pl.pallas_call(
        attend_kernel,
        out_shape=pltpu.VMEM((chunks, piece, HD), first.dtype),
        in_specs=[smem, smem, smem, anywhere, anywhere, vmem],
        out_specs=vmem,
        scratch_shapes=[
            pltpu.VMEM(first.shape, first.dtype),
            pltpu.VMEM((first.shape[0], 2 * HD), first.dtype),
            [pltpu.VMEM(tile, jnp.float32)] * (2 * GROUP),
            [pltpu.VMEM(strip, jnp.float32)] * (2 * GROUP),
            [pltpu.VMEM(tile, jnp.bfloat16)] * (2 * GROUP),
            [pltpu.VMEM(strip, jnp.float32)] * (2 * GROUP),
            pltpu.VMEM((QUERY_TILE, 2 * HD), jnp.float32),
            pltpu.VMEM(strip, jnp.float32),
            pltpu.VMEM((tokens + QUERY_TILE, HD), jnp.float32),
            pltpu.SemaphoreType.DMA((2, SPANS)),
        ],
        compiler_params=pltpu.CompilerParams(vmem_limit_bytes=ATTEND_VMEM),
        name="attend",
    )(meta, gates, items, first, second, queries)


def turned(x, axis, start, length):
    return lax.dynamic_slice_in_dim(jnp.concatenate([x, x], axis=axis), start, length, axis=axis)


def shards(queries, key_rows, value_rows, noise_steps, span_order, token_counts):
    both = ("span", "ctx")
    tok = queries.shape[1]
    piece = tok // 3
    ctx_size = lax.axis_size("ctx")
    me = lax.axis_index("span")
    place = lax.axis_index("ctx")
    turn = place % SPANS
    core = me % 2

    outgoing = pack(turn[None], queries[0], key_rows[0], value_rows[0])
    outgoing = outgoing.reshape(SPANS * HEADS, tok + piece, HD)
    incoming = lax.all_to_all(outgoing, both, split_axis=0, concat_axis=0, tiled=True)

    first = incoming[:, :tok].reshape(SPANS * ctx_size * tok, HD)
    second = lax.ppermute(first, "span", [(0, 1), (1, 0), (2, 3), (3, 2)])
    gates = head_gates(noise_steps, place)
    meta = jnp.concatenate([span_order, token_counts, core[None], me[None]]).astype(jnp.int32)
    out = attend(first, second, incoming, meta, gates)

    back = lax.all_to_all(out, both, split_axis=0, concat_axis=0, tiled=True)
    back = turned(back.reshape(SPANS, HEADS, piece, HD), 0, turn + 1, 3)
    back = back.transpose(0, 2, 1, 3).reshape(tok, HEADS * HD)
    token = place * tok + jnp.arange(tok)
    back = jnp.where((token < token_counts[me])[:, None], back, jnp.zeros((), back.dtype))
    return back[None]


def solution(mesh):
    tokens = P("span", "ctx", None)
    return jax.shard_map(
        shards,
        mesh=mesh,
        in_specs=(tokens, tokens, tokens, P(), P(), P()),
        out_specs=tokens,
        check_vma=False,
    )
```
